256 devices in a mesh: dp: 16 (over z, core), ctx: 16 (over x, y).
Axes of the slice: x: 4, y: 4, z: 8, core: 2. Of those that a mesh axis runs over, the one named last changes fastest.
Arguments:
- qkv: bfloat16 [16, 2048, 12288], P('dp', 'ctx'), may hold values from -6 to 6
- segments: int32 [16, 2048], P('dp'), may hold values from 0 to 7, never falling along the last dimension, each value on 1 to 512 neighbouring positions
- short_taps: float32 [7, 12288], replicated, may hold values from -2.5 to 2.5
- long_taps: bfloat16 [128, 256], replicated, may hold values from -0.5 to 0.5
- cotangent: bfloat16 [16, 2048, 4096], P('dp', 'ctx'), may hold values from -8 to 8
Outputs:
- output: bfloat16 [16, 2048, 4096], P('dp', 'ctx')
- input_grad: bfloat16 [16, 2048, 12288], P('dp', 'ctx')
- short_grad: float32 [7, 12288], replicated
- long_grad: float32 [128, 256], replicated
The draws below stay inside these ranges and needn't reach their ends.
Inputs may be any that keep to these rules, and one draw needn't show every extreme that they name: `segments`: within each pack the document numbers never fall; each of the 8 documents holds 1 to 512 positions, and one holds exactly that many.
All inputs are finite; a program needn't handle non-finite values.
Results may differ from the reference program's by a relative error of at most 0.0076.
Values may be sent and summed in bfloat16 or wider, within the bound.
A program may use at most 192 MiB of HBM per device.

```python
import math
import jax
import jax.numpy as jnp
import numpy as np
from jax import lax

D = 4096
GROUPS = 256
MR_TAPS = 128
SHORT_TAPS = 7
DOCS = 8
PACKS = 16
PACK_LEN = 2048


def draw_cotangent(key, part):
    key = jax.random.fold_in(key, 11)
    first_key = jax.random.fold_in(key, 0)
    position = jnp.arange(PACK_LEN, dtype=jnp.float32) / PACK_LEN
    rising = jnp.exp(jnp.log(3.0) * position)[None, :, None]
    samples = jax.random.normal(first_key, (PACKS, PACK_LEN, D), jnp.float32)
    return jnp.clip(samples * rising, -8.0, 8.0).astype(jnp.bfloat16)


def block_scale(own_key, dims, cuts, smallest, top_value):
    def one(dim, parts):
        steps = jax.random.uniform(jax.random.fold_in(jax.random.fold_in(own_key, 6), dim), (parts,), jnp.float32, smallest / len(cuts), top_value / len(cuts))
        return jnp.repeat(jnp.exp(steps), dims[dim] // parts).reshape((-1,) + (1,) * (len(dims) - dim - 1))

    factor_of = one(*cuts[0])
    for cut in cuts[1:]:
        factor_of = factor_of * one(*cut)
    return factor_of


def split_up(count, total, reach, lean):
    portions = [(1 << 20) // math.isqrt(rank ** lean) + 1 for rank in range(2, count + 1)]
    surplus, given = total - reach - (count - 1), [1] * (count - 1)
    while surplus > 0:
        free = [i for i in range(count - 1) if given[i] < reach]
        pool, left = sum([portions[i] for i in free]), surplus
        for i in free:
            extra = min(reach - given[i], max(1, left * portions[i] // pool), surplus)
            given[i] = given[i] + extra
            surplus = surplus - extra
    return np.array([reach] + given)


def ragged(own_key, count, total, most, lean):
    if count == 2:
        one = jax.random.randint(own_key, (), max(1, total - most), min(most, total - 1) + 1)
        return jnp.stack([one, total - one])
    sizes = jnp.asarray(split_up(count, total, most, lean), jnp.int32)
    pairs = (count - 1) // 2
    source_of, sink = sizes[1:1 + 2 * pairs:2], sizes[2:2 + 2 * pairs:2]
    slack = jnp.minimum(source_of - 1, most - sink)
    passed = jax.random.randint(jax.random.fold_in(own_key, 1), (pairs,), 0, 1 << 20) % (slack + 1)
    sizes = sizes.at[1:1 + 2 * pairs:2].set(source_of - passed).at[2:2 + 2 * pairs:2].set(sink + passed)
    return sizes[jax.random.permutation(jax.random.fold_in(own_key, 2), count)]


def centred(own_key, dims, spread, bound, cuts=(), kind=jnp.bfloat16):
    gain = block_scale(own_key, dims, cuts, -0.22, 0.18) if cuts else 1.0
    entries = jax.random.normal(own_key, dims, jnp.float32) * spread * gain
    return jnp.minimum(jnp.maximum(entries, -bound), bound).astype(kind)


def setup_inputs(seed: int = 0) -> dict:
    arg_keys = jax.random.split(jax.random.key(seed), 6)
    qkv = centred(arg_keys[0], (PACKS, PACK_LEN, 3 * D), 1.0, 6.0, ((0, 16), (1, 16)))
    segments = jax.vmap(lambda own: jnp.searchsorted(jnp.cumsum(ragged(own, DOCS, PACK_LEN, PACK_LEN // 4, 2)), jnp.arange(PACK_LEN), side="right"))(jax.random.split(arg_keys[1], PACKS)).reshape((PACKS, PACK_LEN)).astype(jnp.int32)
    short_taps = centred(arg_keys[2], (SHORT_TAPS, 3 * D), 0.4, 2.5, (), jnp.float32)
    long_taps = centred(arg_keys[3], (MR_TAPS, GROUPS), 0.09, 0.5)
    cotangent = draw_cotangent(jax.random.fold_in(arg_keys[5], 71), 0)
    return dict(qkv=qkv, segments=segments, short_taps=short_taps, long_taps=long_taps, cotangent=cotangent)


def banded(taps_row):
    groups, taps_len = taps_row.shape
    padded = jnp.concatenate([taps_row, jnp.zeros((groups, taps_len), taps_row.dtype)], axis=1)
    tiled = jnp.tile(padded, (1, taps_len))[:, : taps_len * (2 * taps_len - 1)]
    return tiled.reshape(groups, taps_len, 2 * taps_len - 1)


def split_groups(block_rows, groups, group_step):
    per_group = block_rows.shape[1] // groups
    shaped = block_rows.reshape(block_rows.shape[0], groups // group_step, group_step, per_group)
    return jnp.moveaxis(shaped, 1, 0)


def apply_band(taps_row, allowed, block_rows):
    groups, taps_len = taps_row.shape
    group_step = min(groups, 64)
    pieces = split_groups(block_rows.astype(jnp.float32), groups, group_step)
    taps_parts = taps_row.reshape(groups // group_step, group_step, taps_len)

    def one_part(operands):
        taps_part, piece = operands
        matrix = banded(taps_part) * allowed[None]
        return jnp.einsum("gpj,jgc->pgc", matrix, piece, precision=lax.Precision.HIGHEST)

    result = lax.map(one_part, (taps_parts, pieces))
    return jnp.moveaxis(result, 0, 1).reshape(taps_len, block_rows.shape[1])


def lag_block(left_rows, block_rows, allowed, groups):
    taps_len = left_rows.shape[0]
    group_step = min(groups, 64)
    left_parts = split_groups(left_rows.astype(jnp.float32), groups, group_step)
    right_parts = split_groups(block_rows.astype(jnp.float32), groups, group_step)
    inside = banded(jnp.ones((1, taps_len), jnp.float32))[0] * allowed

    def one_part(operands):
        left_part, right_part = operands
        products = jnp.einsum("pgc,jgc->gpj", left_part, right_part, precision=lax.Precision.HIGHEST)
        flattened = (products * inside[None]).reshape(group_step, -1)
        flattened = jnp.concatenate([flattened, jnp.zeros((group_step, taps_len), flattened.dtype)], axis=1)
        return jnp.sum(flattened.reshape(group_step, taps_len, 2 * taps_len)[:, :, :taps_len], axis=1)

    result = lax.map(one_part, (left_parts, right_parts))
    return result.reshape(groups, taps_len)


def block_marks(seg_ext, pack_index, first_row, taps_len, offset):
    marks = lax.dynamic_slice_in_dim(lax.dynamic_index_in_dim(seg_ext, pack_index, 0, False), first_row, 2 * taps_len - 1, 0)
    own_marks = marks[offset:offset + taps_len]
    return (own_marks[:, None] == marks[None, :]).astype(jnp.float32)


def long_apply(extended, seg_ext, taps_row, offset, blocks):
    pack_count = extended.shape[0]
    taps_len = taps_row.shape[1]

    def one_block(block_index):
        pack_index = block_index // blocks
        first_row = (block_index % blocks) * taps_len
        block_rows = lax.dynamic_slice_in_dim(lax.dynamic_index_in_dim(extended, pack_index, 0, False), first_row, 2 * taps_len - 1, 0)
        allowed = block_marks(seg_ext, pack_index, first_row, taps_len, offset)
        return apply_band(taps_row, allowed, block_rows)

    result = lax.map(one_block, jnp.arange(pack_count * blocks, dtype=jnp.int32))
    return result.reshape(pack_count, blocks * taps_len, extended.shape[2])


def long_lags(left_all, extended, seg_ext, groups, taps_len, blocks):
    pack_count = extended.shape[0]

    def one_block(block_index):
        pack_index = block_index // blocks
        first_row = (block_index % blocks) * taps_len
        left_rows = lax.dynamic_slice_in_dim(lax.dynamic_index_in_dim(left_all, pack_index, 0, False), first_row, taps_len, 0)
        block_rows = lax.dynamic_slice_in_dim(lax.dynamic_index_in_dim(extended, pack_index, 0, False), first_row, 2 * taps_len - 1, 0)
        allowed = block_marks(seg_ext, pack_index, first_row, taps_len, taps_len - 1)
        return lag_block(left_rows, block_rows, allowed, groups)

    result = lax.map(one_block, jnp.arange(pack_count * blocks, dtype=jnp.int32))
    return jnp.sum(result, axis=0).T[::-1]


def short_forward(extended, seg_ext, short_taps):
    short_len = short_taps.shape[0]
    shard_rows = extended.shape[1] - short_len + 1
    own_marks = seg_ext[:, short_len - 1:]
    running = jnp.zeros((extended.shape[0], shard_rows, extended.shape[2]), jnp.float32)
    for tap_index in range(short_len):
        source = short_len - 1 - tap_index
        matches = (seg_ext[:, source:source + shard_rows] == own_marks).astype(jnp.float32)[..., None]
        running = running + short_taps[tap_index] * (extended[:, source:source + shard_rows].astype(jnp.float32) * matches)
    return running


def short_backward(extended, seg_ext, short_taps):
    short_len = short_taps.shape[0]
    shard_rows = extended.shape[1] - short_len + 1
    own_marks = seg_ext[:, :shard_rows]
    running = jnp.zeros((extended.shape[0], shard_rows, extended.shape[2]), jnp.float32)
    for tap_index in range(short_len):
        matches = (seg_ext[:, tap_index:tap_index + shard_rows] == own_marks).astype(jnp.float32)[..., None]
        running = running + short_taps[tap_index] * (extended[:, tap_index:tap_index + shard_rows].astype(jnp.float32) * matches)
    return running


def short_terms(branch_grad, extended, seg_ext, short_len):
    shard_rows = branch_grad.shape[1]
    own_marks = seg_ext[:, short_len - 1:]
    upstream = branch_grad.astype(jnp.float32)
    collected = []
    for tap_index in range(short_len):
        source = short_len - 1 - tap_index
        matches = (seg_ext[:, source:source + shard_rows] == own_marks).astype(jnp.float32)[..., None]
        collected.append(jnp.sum(upstream * extended[:, source:source + shard_rows].astype(jnp.float32) * matches, axis=(0, 1)))
    return jnp.stack(collected, axis=0)


def reference(qkv, segments, short_taps, long_taps, cotangent):
    taps_len = long_taps.shape[0]
    groups = long_taps.shape[1]
    short_len = short_taps.shape[0]
    channels = cotangent.shape[2]
    taps_wide = long_taps.astype(jnp.float32)

    def one_pack(operands):
        inputs, marks, upstream = operands
        inputs = inputs[None]
        marks = marks[None]
        upstream = upstream[None]
        shard_rows = inputs.shape[1]
        blocks = shard_rows // taps_len
        padding = -jnp.ones((1, taps_len - 1), jnp.int32)
        window = jnp.concatenate([padding, marks.astype(jnp.int32), padding], axis=1)
        seg_fwd = window[:, : shard_rows + taps_len - 1]
        seg_bwd = window[:, taps_len - 1:]
        seg_sfwd = window[:, taps_len - short_len: taps_len - 1 + shard_rows]
        seg_sbwd = window[:, taps_len - 1: taps_len - 1 + shard_rows + short_len - 1]
        before = jnp.zeros((1, short_len - 1, 3 * channels), jnp.bfloat16)
        input_ext = jnp.concatenate([before, inputs], axis=1)
        short_out = short_forward(input_ext, seg_sfwd, short_taps).astype(jnp.bfloat16)
        query_part = short_out[..., :channels].astype(jnp.float32)
        key_rows = short_out[..., channels:2 * channels].astype(jnp.float32)
        value_rows = short_out[..., 2 * channels:].astype(jnp.float32)
        product = (key_rows * value_rows).astype(jnp.bfloat16)
        product_ext = jnp.concatenate([jnp.zeros((1, taps_len - 1, channels), jnp.bfloat16), product], axis=1)
        mixing = long_apply(product_ext, seg_fwd, taps_wide.T[:, ::-1], taps_len - 1, blocks)
        output = (query_part * mixing).astype(jnp.bfloat16)
        upstream_f32 = upstream.astype(jnp.float32)
        gate_grad = (upstream_f32 * query_part).astype(jnp.bfloat16)
        query_grad = upstream_f32 * mixing
        grad_ext = jnp.concatenate([gate_grad, jnp.zeros((1, taps_len - 1, channels), jnp.bfloat16)], axis=1)
        product_grad = long_apply(grad_ext, seg_bwd, taps_wide.T, 0, blocks)
        branch_grad = jnp.concatenate([query_grad, product_grad * value_rows, product_grad * key_rows], axis=2).astype(jnp.bfloat16)
        branch_ext = jnp.concatenate([branch_grad, jnp.zeros((1, short_len - 1, 3 * channels), jnp.bfloat16)], axis=1)
        input_grad = short_backward(branch_ext, seg_sbwd, short_taps).astype(jnp.bfloat16)
        short_sum = short_terms(branch_grad, input_ext, seg_sfwd, short_len)
        long_sum = long_lags(gate_grad, product_ext, seg_fwd, groups, taps_len, blocks)
        return output[0], input_grad[0], short_sum, long_sum

    results = lax.map(one_pack, (qkv, segments, cotangent))
    return results[0], results[1], jnp.sum(results[2], axis=0), jnp.sum(results[3], axis=0)
```

```python
import functools

import jax
import jax.numpy as jnp
from jax import lax
from jax.experimental import pallas as pl
from jax.experimental.pallas import tpu as pltpu
from jax.sharding import PartitionSpec as P

MESH = pl.DeviceIdType.MESH
L = 128
D = 4096
TILES = D // L
W = 512
CHUNKS = D // W
U = W // L
SHORT = 7
GT = 4 * TILES
F32 = jnp.float32
BF16 = jnp.bfloat16


def kernel(nz, nctx, qkv, segs, staps, ltaps, cot, out, ig, sgo, lgo,
           hq_out, hq_in, prod, gg, short, bg, bg_out, bg_in, xs, fwd_mask, bwd_mask,
           mf, mb, mtri, seg_col, hf, hb, lane_sel, lhs_f, lhs_b, lhs_g, res_f, res_b, res_g, lag_rows,
           grads, part, half, zpart, total,
           send, recv, asend, arecv, psend, precv, zsend, zrecv, p2send, p2recv, gsend, grecv):
    dp, ctx = lax.axis_index("dp"), lax.axis_index("ctx")
    left, right = lax.rem(ctx + nctx - 1, nctx), lax.rem(ctx + 1, nctx)
    core = lax.rem(dp, 2)
    z = dp // 2
    twin = dp + 1 - 2 * core
    per = GT // nctx
    hper = per // 2

    barrier = pltpu.get_barrier_semaphore()

    def greet_ctx(k, c):
        pl.semaphore_signal(barrier, inc=1, device_id=(dp, lax.rem(ctx + k, nctx)), device_id_type=MESH)
        return c

    def greet_z(k, c):
        pl.semaphore_signal(barrier, inc=1, device_id=(lax.rem(z + k, nz) * 2 + core, ctx), device_id_type=MESH)
        return c

    lax.fori_loop(1, nctx, greet_ctx, 0)
    lax.fori_loop(1, nz, greet_z, 0)
    pl.semaphore_signal(barrier, inc=1, device_id=(twin, ctx), device_id_type=MESH)

    def pack(c, carry):
        for u in range(U):
            lane = pl.multiple_of(c * W + u * L, L)
            rows = [qkv[112:128, pl.ds(s * D + lane, L)].astype(F32)[8:16] for s in range(3)]
            hq_out[c, 0:16, u * L:(u + 1) * L] = jnp.concatenate(rows[0:2], 0).astype(BF16)
            hq_out[c, 16:32, u * L:(u + 1) * L] = jnp.concatenate([rows[2], rows[2]], 0).astype(BF16)
        return carry

    lax.fori_loop(0, CHUNKS, pack, 0)
    pl.semaphore_wait(barrier, nctx + nz - 1)

    def hq_copy(c):
        return pltpu.make_async_remote_copy(hq_out.at[c], hq_in.at[c], send.at[0, c], recv.at[0, c], device_id=(dp, right), device_id_type=MESH)

    def prod_copy(c):
        return pltpu.make_async_remote_copy(prod.at[c, pl.ds(L, L)], prod.at[c, pl.ds(0, L)], send.at[1, c], recv.at[1, c], device_id=(dp, right), device_id_type=MESH)

    def gg_copy(c):
        return pltpu.make_async_remote_copy(gg.at[c, pl.ds(0, L)], gg.at[c, pl.ds(L, L)], send.at[2, c], recv.at[2, c], device_id=(dp, left), device_id_type=MESH)

    def bg_copy(c):
        return pltpu.make_async_remote_copy(bg_out.at[c], bg_in.at[c], send.at[3, c], recv.at[3, c], device_id=(dp, left), device_id_type=MESH)

    def go(copy):
        def step(c, carry):
            copy(c).start()
            return carry
        return step

    lax.fori_loop(0, CHUNKS, go(hq_copy), 0)

    own = segs[0:1, pl.ds(pl.multiple_of(ctx * L, L), L)].astype(F32)
    prev = segs[0:1, pl.ds(pl.multiple_of(left * L, L), L)].astype(F32)
    nxt = segs[0:1, pl.ds(pl.multiple_of(right * L, L), L)].astype(F32)
    prev = jnp.where(ctx == 0, -1.0, prev)
    nxt = jnp.where(ctx == nctx - 1, -1.0, nxt)
    own_r = jnp.broadcast_to(own, (L, L))
    prev_r = jnp.broadcast_to(prev, (L, L))
    next_r = jnp.broadcast_to(nxt, (L, L))
    own_c = own_r.T
    seg_col[0:8] = prev_r.T[120:128]
    seg_col[8:136] = own_c
    seg_col[136:144] = next_r.T[0:8]
    rows = lax.broadcasted_iota(jnp.int32, (L, L), 0)
    cols = lax.broadcasted_iota(jnp.int32, (L, L), 1)
    same_own = own_c == own_r
    one = jnp.ones((L, L), F32)
    zero = jnp.zeros((L, L), F32)
    mf[:, 0:L] = jnp.where(jnp.logical_and(own_c == prev_r, rows < cols), one, zero).astype(BF16)
    mf[:, L:2 * L] = jnp.where(jnp.logical_and(same_own, rows >= cols), one, zero).astype(BF16)
    b_own = jnp.where(jnp.logical_and(same_own, cols >= rows), one, zero)
    b_next = jnp.where(jnp.logical_and(own_c == next_r, cols < rows), one, zero)
    mb[:, 0:L] = b_own.astype(BF16)
    mb[:, L:2 * L] = b_next.astype(BF16)
    mtri[0] = b_own
    mtri[1] = b_next
    for t in range(1, SHORT):
        fwd_mask[t - 1] = jnp.where(own_c == seg_col[8 - t:136 - t], one, zero)
        bwd_mask[t - 1] = jnp.where(own_c == seg_col[8 + t:136 + t], one, zero)
    eye = jnp.where(rows == cols, one, zero).astype(BF16)
    back = jnp.where(jnp.logical_or(rows + cols == L, rows + cols == 0), one, zero).astype(BF16)
    dims = (((0,), (0,)), ((), ()))
    hb[...] = lax.dot_general(ltaps[...], eye, dims, preferred_element_type=F32).reshape(TILES, 8, L)
    hf[...] = lax.dot_general(ltaps[...], back, dims, preferred_element_type=F32).reshape(TILES, 8, L)
    for g in range(8):
        lane_sel[g] = jnp.where(cols // 16 == g, one, zero).astype(BF16)

    def first(c, carry):
        hq_copy(c).wait_recv()

        def tile(u, carry):
            lane = pl.multiple_of(u * L, L)
            wide = pl.multiple_of(c * W + u * L, L)
            halo_a = hq_in[c, 0:16, pl.ds(lane, L)].astype(F32)
            halo_b = hq_in[c, 16:32, pl.ds(lane, L)].astype(F32)
            halos = (halo_a[0:8], halo_a[8:16], halo_b[0:8])
            done = []
            for s in range(3):
                at = pl.ds(s * D + wide, L)
                x = qkv[:, at].astype(F32)
                xs[s, 0:8] = halos[s]
                xs[s, 8:136] = x
                y = staps[0:1, at] * x
                for t in range(1, SHORT):
                    y = y + staps[t:t + 1, at] * (xs[s, 8 - t:136 - t] * fwd_mask[t - 1])
                y = y.astype(BF16)
                short[s, :, pl.ds(wide, L)] = y
                done.append(y.astype(F32))
            prod[c, L:2 * L, pl.ds(lane, L)] = (done[1] * done[2]).astype(BF16)
            gg[c, 0:L, pl.ds(lane, L)] = (cot[:, pl.ds(wide, L)].astype(F32) * done[0]).astype(BF16)
            return carry

        lax.fori_loop(0, U, tile, 0)
        prod_copy(c).start()
        gg_copy(c).start()
        return carry

    lax.fori_loop(0, CHUNKS, first, 0)

    lane_id = lax.broadcasted_iota(jnp.int32, (L, L), 1) // 16

    def second(c, carry):
        prod_copy(c).wait_recv()
        gg_copy(c).wait_recv()

        def tile(u, carry):
            lane = pl.multiple_of(u * L, L)
            n = c * U + u
            wide = pl.multiple_of(n * L, L)
            p_ext = prod[c, :, pl.ds(lane, L)]
            g_ext = gg[c, :, pl.ds(lane, L)]
            p_own = p_ext[L:2 * L]
            taps_f = hf[n]
            taps_b = hb[n]
            for g in range(8):
                ring = pltpu.roll(jnp.broadcast_to(taps_f[g:g + 1], (L, L)), 0, 1, stride=1, stride_axis=0).astype(BF16)
                lhs_f[g * L:(g + 1) * L, 0:L] = ring * mf[:, 0:L]
                lhs_f[g * L:(g + 1) * L, L:2 * L] = ring * mf[:, L:2 * L]
                ring = pltpu.roll(jnp.broadcast_to(taps_b[g:g + 1], (L, L)), 0, 1, stride=1, stride_axis=0).astype(BF16)
                lhs_b[g * L:(g + 1) * L, 0:L] = ring * mb[:, 0:L]
                lhs_b[g * L:(g + 1) * L, L:2 * L] = ring * mb[:, L:2 * L]
                lhs_g[g * L:(g + 1) * L] = p_own * lane_sel[g]
            res_f[...] = jnp.dot(lhs_f[...], p_ext, preferred_element_type=F32)
            res_b[...] = jnp.dot(lhs_b[...], g_ext, preferred_element_type=F32)
            res_g[...] = lax.dot_general(lhs_g[...], g_ext, (((1,), (1,)), ((), ())), preferred_element_type=F32)
            mix = res_f[0:L]
            pg = res_b[0:L]
            for g in range(1, 8):
                mix = jnp.where(lane_id == g, res_f[g * L:(g + 1) * L], mix)
                pg = jnp.where(lane_id == g, res_b[g * L:(g + 1) * L], pg)
            for g in range(8):
                acc = None
                for k in range(16):
                    r = slice(g * L + 8 * k, g * L + 8 * k + 8)
                    kk = slice(8 * k, 8 * k + 8)
                    block = res_g[r, 0:L] * mtri[0, kk] + res_g[r, L:2 * L] * mtri[1, kk]
                    if k:
                        block = pltpu.roll(block, L - 8 * k, 1)
                    acc = block if acc is None else acc + block
                lag_rows[g] = acc
            lags = lag_rows[:, 0, :]
            for k in range(1, 8):
                lags = lags + pltpu.roll(lag_rows[:, k, :], L - k, 1)
            grads[3 * TILES + n] = lags
            q = short[0, :, pl.ds(wide, L)].astype(F32)
            k = short[1, :, pl.ds(wide, L)].astype(F32)
            v = short[2, :, pl.ds(wide, L)].astype(F32)
            out[:, pl.ds(wide, L)] = (q * mix).astype(BF16)
            up = cot[:, pl.ds(wide, L)].astype(F32)
            b = [(x).astype(BF16).astype(F32) for x in (up * mix, pg * v, pg * k)]
            for s in range(3):
                bg[s * TILES + n, 0:L] = b[s]
            bg_out[c, 0:16, pl.ds(lane, L)] = jnp.concatenate([b[0][0:8], b[1][0:8]], 0).astype(BF16)
            bg_out[c, 16:32, pl.ds(lane, L)] = jnp.concatenate([b[2][0:8], b[2][0:8]], 0).astype(BF16)
            return carry

        lax.fori_loop(0, U, tile, 0)
        bg_copy(c).start()
        return carry

    def third(c, carry):
        bg_copy(c).wait_recv()

        def tile(u, carry):
            lane = pl.multiple_of(u * L, L)
            n = c * U + u
            wide = pl.multiple_of(n * L, L)
            halo_a = bg_in[c, 0:16, pl.ds(lane, L)].astype(F32)
            halo_b = bg_in[c, 16:32, pl.ds(lane, L)].astype(F32)
            halos = (halo_a[0:8], halo_a[8:16], halo_b[0:8])
            for s in range(3):
                m = s * TILES + n
                at = pl.ds(s * D + wide, L)
                bg[m, L:L + 8] = halos[s]
                x = qkv[:, at].astype(F32)
                b = bg[m, 0:L]
                y = staps[0:1, at] * b
                terms = [jnp.sum(x * b, axis=0, keepdims=True)]
                for t in range(1, SHORT):
                    b = bg[m, t:L + t] * bwd_mask[t - 1]
                    y = y + staps[t:t + 1, at] * b
                    terms.append(jnp.sum(x * b, axis=0, keepdims=True))
                ig[:, at] = y.astype(BF16)
                terms.append(jnp.zeros((1, L), F32))
                grads[m] = jnp.concatenate(terms, 0)
            return carry

        lax.fori_loop(0, U, tile, 0)
        return carry

    def both(c, carry):
        second(c, carry)

        @pl.when(c > 0)
        def _():
            third(c - 1, carry)

        return carry

    lax.fori_loop(0, CHUNKS, both, 0)
    third(CHUNKS - 1, 0)

    def scatter_copy(k):
        to = lax.rem(ctx + k, nctx)
        return pltpu.make_async_remote_copy(grads.at[pl.ds(to * per, per)], part.at[k], asend.at[k], arecv.at[k], device_id=(dp, to), device_id_type=MESH)

    lax.fori_loop(1, nctx, go(scatter_copy), 0)

    def gather_sum(k, acc):
        scatter_copy(k).wait_recv()
        return acc + part[k]

    half[0] = lax.fori_loop(1, nctx, gather_sum, grads[pl.ds(ctx * per, per)])
    pair = pltpu.make_async_remote_copy(half.at[0, pl.ds((1 - core) * hper, hper)], half.at[1, pl.ds(0, hper)], psend, precv, device_id=(twin, ctx), device_id_type=MESH)
    pair.start()
    pair.wait_recv()
    zpart[z] = half[0, pl.ds(core * hper, hper)] + half[1, 0:hper]

    def z_copy(k):
        return pltpu.make_async_remote_copy(zpart.at[z], zpart.at[z], zsend.at[k], zrecv.at[k], device_id=(lax.rem(z + k, nz) * 2 + core, ctx), device_id_type=MESH)

    def z_wait(k, carry):
        src = lax.rem(z + nz - k, nz)
        pltpu.make_async_remote_copy(zpart.at[src], zpart.at[src], zsend.at[k], zrecv.at[k], device_id=(lax.rem(z + k, nz) * 2 + core, ctx), device_id_type=MESH).wait_recv()
        return carry

    lax.fori_loop(1, nz, go(z_copy), 0)
    lax.fori_loop(1, nz, z_wait, 0)
    mine = zpart[0]
    for k in range(1, nz):
        mine = mine + zpart[k]
    base = ctx * per
    at = pl.ds(base + core * hper, hper)
    total[at] = mine
    pair2 = pltpu.make_async_remote_copy(total.at[at], total.at[at], p2send, p2recv, device_id=(twin, ctx), device_id_type=MESH)
    pair2.start()
    other = pl.ds(base + (1 - core) * hper, hper)
    pltpu.make_async_remote_copy(total.at[other], total.at[other], p2send, p2recv, device_id=(twin, ctx), device_id_type=MESH).wait_recv()

    def gather_copy(k):
        block = total.at[pl.ds(base, per)]
        return pltpu.make_async_remote_copy(block, block, gsend.at[k], grecv.at[k], device_id=(dp, lax.rem(ctx + k, nctx)), device_id_type=MESH)

    def gather_wait(k, carry):
        src = lax.rem(ctx + nctx - k, nctx)
        block = total.at[pl.ds(src * per, per)]
        pltpu.make_async_remote_copy(block, block, gsend.at[k], grecv.at[k], device_id=(dp, lax.rem(ctx + k, nctx)), device_id_type=MESH).wait_recv()
        return carry

    lax.fori_loop(1, nctx, go(gather_copy), 0)
    lax.fori_loop(1, nctx, gather_wait, 0)
    for n in range(3 * TILES):
        sgo[:, n * L:(n + 1) * L] = total[n][0:SHORT]
    lgo[...] = total[3 * TILES:].reshape(8 * TILES, L).T

    def drain(copy):
        def step(c, carry):
            copy(c).wait_send()
            return carry
        return step

    for copy in (hq_copy, prod_copy, gg_copy, bg_copy):
        lax.fori_loop(0, CHUNKS, drain(copy), 0)
    lax.fori_loop(1, nctx, drain(scatter_copy), 0)
    lax.fori_loop(1, nz, drain(z_copy), 0)
    lax.fori_loop(1, nctx, drain(gather_copy), 0)
    pair.wait_send()
    pair2.wait_send()


def body(nz, nctx, qkv, segments, short_taps, long_taps, cotangent):
    per = GT // nctx
    vmem = pl.BlockSpec(memory_space=pltpu.VMEM)
    dma = pltpu.SemaphoreType.DMA
    shape = jax.ShapeDtypeStruct
    out, ig, sg, lg = pl.pallas_call(
        functools.partial(kernel, nz, nctx),
        out_shape=(shape((L, D), BF16), shape((L, 3 * D), BF16), shape((SHORT, 3 * D), F32), shape((L, 8 * TILES), F32)),
        in_specs=[vmem] * 5,
        out_specs=[vmem] * 4,
        scratch_shapes=[
            pltpu.VMEM((CHUNKS, 32, W), BF16),
            pltpu.VMEM((CHUNKS, 32, W), BF16),
            pltpu.VMEM((CHUNKS, 2 * L, W), BF16),
            pltpu.VMEM((CHUNKS, 2 * L, W), BF16),
            pltpu.VMEM((3, L, D), BF16),
            pltpu.VMEM((3 * TILES, L + 8, L), F32),
            pltpu.VMEM((CHUNKS, 32, W), BF16),
            pltpu.VMEM((CHUNKS, 32, W), BF16),
            pltpu.VMEM((3, L + 8, L), F32),
            pltpu.VMEM((SHORT - 1, L, L), F32),
            pltpu.VMEM((SHORT - 1, L, L), F32),
            pltpu.VMEM((L, 2 * L), BF16),
            pltpu.VMEM((L, 2 * L), BF16),
            pltpu.VMEM((2, L, L), F32),
            pltpu.VMEM((L + 16, L), F32),
            pltpu.VMEM((TILES, 8, L), F32),
            pltpu.VMEM((TILES, 8, L), F32),
            pltpu.VMEM((8, L, L), BF16),
            pltpu.VMEM((8 * L, 2 * L), BF16),
            pltpu.VMEM((8 * L, 2 * L), BF16),
            pltpu.VMEM((8 * L, L), BF16),
            pltpu.VMEM((8 * L, L), F32),
            pltpu.VMEM((8 * L, L), F32),
            pltpu.VMEM((8 * L, 2 * L), F32),
            pltpu.VMEM((8, 8, L), F32),
            pltpu.VMEM((GT, 8, L), F32),
            pltpu.VMEM((nctx, per, 8, L), F32),
            pltpu.VMEM((2, per, 8, L), F32),
            pltpu.VMEM((nz, per // 2, 8, L), F32),
            pltpu.VMEM((GT, 8, L), F32),
            dma((4, CHUNKS)), dma((4, CHUNKS)),
            dma((nctx,)), dma((nctx,)),
            dma, dma,
            dma((nz,)), dma((nz,)),
            dma, dma,
            dma((nctx,)), dma((nctx,)),
        ],
        compiler_params=pltpu.CompilerParams(collective_id=0, has_side_effects=True, vmem_limit_bytes=56 * 1024 * 1024),
        cost_estimate=pl.CostEstimate(flops=20_000_000_000, bytes_accessed=10_000_000, transcendentals=0),
        name="hyena",
    )(qkv[0], segments, short_taps, long_taps, cotangent[0])
    return out[None], ig[None], sg, lg


def solution(mesh):
    in_specs = (P("dp", "ctx", None), P("dp", None), P(), P(), P("dp", "ctx", None))
    out_specs = (P("dp", "ctx", None), P("dp", "ctx", None), P(), P())
    step = functools.partial(body, mesh.shape["dp"] // 2, mesh.shape["ctx"])
    return jax.shard_map(step, mesh=mesh, in_specs=in_specs, out_specs=out_specs, check_vma=False)
```

```python
import functools

import jax
import jax.numpy as jnp
from jax import lax
from jax.experimental import pallas as pl
from jax.experimental.pallas import tpu as pltpu
from jax.sharding import PartitionSpec as P

MESH = pl.DeviceIdType.MESH
L = 128
D = 4096
TILES = D // L
W = 256
CHUNKS = D // W
U = W // L
SHORT = 7
H = 16
SIDE = 4
SUPER = CHUNKS // 2
SPANS = ((0, 4), (4, 4))
LOOP_STAGES = ((11, "a", 0), (12, "b", 0), (14, "c", 0), (15, "d", 0))
PART = 4
EARLY = 8
AHEAD = 3
ROWS = 16
LAG = 4
F32 = jnp.float32
BF16 = jnp.bfloat16


def kernel(nz, qkv_hbm, segs_hbm, staps_hbm, ltaps_hbm, cot_hbm, out_hbm, ig_hbm, sgo, lgo,
           qkv, segs, staps, ltaps, cot, out, ig, hq_out, hq_in, prod, gg, short, bg, bg_out, bg_in, xs, xh, fwd_mask, bwd_mask,
           mf, mb, mtri, seg_col, hf, hb, lane_sel, lag_rows, lag_all,
           grads, twin_in, z_in, y_in, x_in, total,
           load, store, hsend, hrecv, psend, precv, csend, crecv, bsend, brecv, tsend, trecv, rsend, rrecv, ysend, yrecv, xsend, xrecv, gsend, grecv):
    nctx, ndp = SIDE * SIDE, 2 * nz
    dp, ctx = lax.axis_index("dp"), lax.axis_index("ctx")
    core, z = lax.rem(dp, 2), dp // 2
    left, right = lax.rem(ctx + nctx - 1, nctx), lax.rem(ctx + 1, nctx)
    my_x, my_y = ctx // SIDE, lax.rem(ctx, SIDE)
    y_at = [my_x * SIDE + lax.rem(my_y + k, SIDE) for k in range(SIDE)]
    x_at = [lax.rem(my_x + k, SIDE) * SIDE + my_y for k in range(SIDE)]

    loads = [pltpu.make_async_copy(src, dst, load.at[i]) for i, (src, dst) in enumerate(
        ((segs_hbm, segs), (ltaps_hbm, ltaps), (staps_hbm, staps), (qkv_hbm, qkv), (cot_hbm, cot)))]
    for one_load in loads:
        one_load.start()

    barrier = pltpu.get_barrier_semaphore()

    def greet_dp(k, c):
        pl.semaphore_signal(barrier, inc=1, device_id=(lax.rem(dp + k, ndp), ctx), device_id_type=MESH)
        return c

    lax.fori_loop(1, ndp, greet_dp, 0)
    for to in [left, right] + y_at[1:] + x_at[1:]:
        pl.semaphore_signal(barrier, inc=1, device_id=(dp, to), device_id_type=MESH)

    def hop(src, dst, s, r, to):
        return pltpu.make_async_remote_copy(src, dst, s, r, device_id=(dp, to), device_id_type=MESH)

    def part(i):
        return pl.ds(i * PART, PART)

    def hq_copy(i):
        return hop(hq_out.at[part(i)], hq_in.at[part(i)], hsend.at[0, i], hrecv.at[0, i], right)

    def prod_head(i):
        return hop(prod.at[part(i), pl.ds(L, H)], prod.at[part(i), pl.ds(0, H)], hsend.at[1, i], hrecv.at[1, i], right)

    def gg_head(i):
        return hop(gg.at[part(i), pl.ds(0, H)], gg.at[part(i), pl.ds(L, H)], hsend.at[2, i], hrecv.at[2, i], left)

    def prod_copy(c):
        return hop(prod.at[c, pl.ds(L + H, L - H)], prod.at[c, pl.ds(H, L - H)], psend.at[c], precv.at[c], right)

    def gg_copy(c):
        return hop(gg.at[c, pl.ds(H, L - H)], gg.at[c, pl.ds(L + H, L - H)], csend.at[c], crecv.at[c], left)

    def bg_copy(c):
        return hop(bg_out.at[c], bg_in.at[c], bsend.at[c], brecv.at[c], left)

    def out_copy(c):
        at = pl.ds(pl.multiple_of(c * W, W), W)
        return pltpu.make_async_copy(out.at[:, at], out_hbm.at[:, at], store.at[0, c])

    def ig_copy(c, s):
        at = pl.ds(pl.multiple_of(s * D + c * W, W), W)
        return pltpu.make_async_copy(ig.at[:, at], ig_hbm.at[:, at], store.at[1 + s, c])

    loads[0].wait()
    own = segs[0:1, pl.ds(pl.multiple_of(ctx * L, L), L)].astype(F32)
    prev = segs[0:1, pl.ds(pl.multiple_of(left * L, L), L)].astype(F32)
    nxt = segs[0:1, pl.ds(pl.multiple_of(right * L, L), L)].astype(F32)
    prev = jnp.where(ctx == 0, -1.0, prev)
    nxt = jnp.where(ctx == nctx - 1, -1.0, nxt)
    own_r = jnp.broadcast_to(own, (L, L))
    prev_r = jnp.broadcast_to(prev, (L, L))
    next_r = jnp.broadcast_to(nxt, (L, L))
    own_c = own_r.T
    seg_col[0:8] = prev_r.T[120:128]
    seg_col[8:136] = own_c
    seg_col[136:144] = next_r.T[0:8]
    rows = lax.broadcasted_iota(jnp.int32, (L, L), 0)
    cols = lax.broadcasted_iota(jnp.int32, (L, L), 1)
    same_own = own_c == own_r
    one = jnp.ones((L, L), F32)
    zero = jnp.zeros((L, L), F32)
    mf[:, 0:L] = jnp.where(jnp.logical_and(own_c == prev_r, rows < cols), one, zero).astype(BF16)
    mf[:, L:2 * L] = jnp.where(jnp.logical_and(same_own, rows >= cols), one, zero).astype(BF16)
    b_own = jnp.where(jnp.logical_and(same_own, cols >= rows), one, zero)
    b_next = jnp.where(jnp.logical_and(own_c == next_r, cols < rows), one, zero)
    mb[:, 0:L] = b_own.astype(BF16)
    mb[:, L:2 * L] = b_next.astype(BF16)
    mtri[0] = b_own
    mtri[1] = b_next
    for t in range(1, SHORT):
        fwd_mask[t - 1] = jnp.where(own_c == seg_col[8 - t:136 - t], one, zero)
        bwd_mask[t - 1] = jnp.where(own_c == seg_col[8 + t:136 + t], one, zero)
    loads[1].wait()
    eye = jnp.where(rows == cols, one, zero).astype(BF16)
    back = jnp.where(jnp.logical_or(rows + cols == L, rows + cols == 0), one, zero).astype(BF16)
    dims = (((0,), (0,)), ((), ()))
    hb[...] = lax.dot_general(ltaps[...], eye, dims, preferred_element_type=F32).reshape(TILES, 8, L)
    hf[...] = lax.dot_general(ltaps[...], back, dims, preferred_element_type=F32).reshape(TILES, 8, L)
    for g in range(8):
        lane_sel[g] = jnp.where(cols // 16 == g, one, zero).astype(BF16)
    lane_id = cols // 16

    for one_load in loads[2:]:
        one_load.wait()

    def pack(dst, c, parts):
        flat = [parts[u][s] for u in range(U) for s in range(3)]
        for k in range(0, 3 * U, 2):
            dst[c, 8 * k:8 * k + 16] = jnp.concatenate(flat[k:k + 2], 0).astype(BF16)

    def unpack(src, c):
        flat = []
        for k in range(0, 3 * U, 2):
            two = src[c, 8 * k:8 * k + 16].astype(F32)
            flat += [two[0:8], two[8:16]]
        return [flat[3 * u:3 * u + 3] for u in range(U)]

    def lanes(c, u):
        return pl.multiple_of(c * W + u * L, L)

    def pack_last(c, carry):
        pack(hq_out, c, [[qkv[L - 16:L, pl.ds(s * D + lanes(c, u), L)].astype(F32)[8:16] for s in range(3)] for u in range(U)])
        return carry

    lax.fori_loop(0, CHUNKS, pack_last, 0)

    def gates(c, u, r0, r1, done):
        here = slice(u * L, (u + 1) * L)
        wide = pl.ds(lanes(c, u), L)
        y = [d.astype(BF16) for d in done]
        for s in range(3):
            short[s, r0:r1, wide] = y[s]
        q, k, v = [d.astype(F32) for d in y]
        prod[c, L + r0:L + r1, here] = (k * v).astype(BF16)
        gg[c, r0:r1, here] = (cot[r0:r1, wide].astype(F32) * q).astype(BF16)

    def first(c, carry):
        for u in range(U):
            done = []
            for s in range(3):
                at = pl.ds(s * D + lanes(c, u), L)
                k = u * 3 + s
                x = qkv[:, at].astype(F32)
                xs[k] = x
                y = staps[0:1, at] * x[H:L]
                for t in range(1, SHORT):
                    y = y + staps[t:t + 1, at] * (xs[k, H - t:L - t] * fwd_mask[t - 1, H:L])
                done.append(y)
            gates(c, u, H, L, done)
        return carry

    lax.fori_loop(0, EARLY, first, 0)
    pl.semaphore_wait(barrier, ndp - 1 + 2 + 2 * (SIDE - 1))
    for i in range(CHUNKS // PART):
        hq_copy(i).start()
    for c in range(AHEAD):
        gg_copy(c).start()
    lax.fori_loop(EARLY, CHUNKS, first, 0)
    for c in range(AHEAD):
        prod_copy(c).start()

    def first_rows(c, carry):
        halos = unpack(hq_in, c)
        for u in range(U):
            done = []
            for s in range(3):
                at = pl.ds(s * D + lanes(c, u), L)
                k = u * 3 + s
                x = qkv[0:H, at].astype(F32)
                xh[k, 0:8] = halos[u][s]
                xh[k, 8:8 + H] = x
                y = staps[0:1, at] * x
                for t in range(1, SHORT):
                    y = y + staps[t:t + 1, at] * (xh[k, 8 - t:8 + H - t] * fwd_mask[t - 1, 0:H])
                done.append(y)
            gates(c, u, 0, H, done)
        return carry

    def first_part(i, carry):
        hq_copy(i).wait_recv()
        lax.fori_loop(i * PART, (i + 1) * PART, first_rows, 0)
        prod_head(i).start()
        gg_head(i).start()
        return carry

    lax.fori_loop(0, CHUNKS // PART, first_part, 0)

    def second(c):
        parts = []
        for u in range(U):
            here = slice(u * L, (u + 1) * L)
            n = c * U + u
            wide = pl.ds(lanes(c, u), L)
            p_ext = prod[c, :, here]
            g_ext = gg[c, :, here]
            p_own = p_ext[L:2 * L]
            taps_f = hf[n]
            taps_b = hb[n]
            mix = pg = None
            for g in range(8):
                rf = pltpu.roll(jnp.broadcast_to(taps_f[g:g + 1], (L, L)), 0, 1, stride=1, stride_axis=0).astype(BF16)
                rb = pltpu.roll(jnp.broadcast_to(taps_b[g:g + 1], (L, L)), 0, 1, stride=1, stride_axis=0).astype(BF16)
                lf = jnp.concatenate([rf * mf[:, 0:L], rf * mf[:, L:2 * L]], 1)
                lb = jnp.concatenate([rb * mb[:, 0:L], rb * mb[:, L:2 * L]], 1)
                r1 = jnp.dot(lf, p_ext, preferred_element_type=F32)
                r2 = jnp.dot(lb, g_ext, preferred_element_type=F32)
                rg = lax.dot_general(p_own * lane_sel[g], g_ext, (((1,), (1,)), ((), ())), preferred_element_type=F32)
                mix = r1 if mix is None else jnp.where(lane_id == g, r1, mix)
                pg = r2 if pg is None else jnp.where(lane_id == g, r2, pg)
                acc = None
                for k in range(16):
                    r = slice(8 * k, 8 * k + 8)
                    block = rg[r, 0:L] * mtri[0, r] + rg[r, L:2 * L] * mtri[1, r]
                    if k:
                        block = pltpu.roll(block, L - 8 * k, 1)
                    acc = block if acc is None else acc + block
                lag_rows[u, g] = acc
            lags = lag_rows[u, :, 0, :]
            for k in range(1, 8):
                lags = lags + pltpu.roll(lag_rows[u, :, k, :], L - k, 1)
            grads[12 + lax.rem(c, 2) * U + u, c // 2] = lags
            q = short[0, :, wide].astype(F32)
            k = short[1, :, wide].astype(F32)
            v = short[2, :, wide].astype(F32)
            out[:, wide] = (q * mix).astype(BF16)
            up = cot[:, wide].astype(F32)
            b = [x.astype(BF16).astype(F32) for x in (up * mix, pg * v, pg * k)]
            for s in range(3):
                bg[c, u * 3 + s, 0:L] = b[s]
            parts.append([x[0:8] for x in b])
        pack(bg_out, c, parts)

    def third(c):
        halos = unpack(bg_in, c)
        for u in range(U):
            for s in range(3):
                bg[c, u * 3 + s, L:L + 8] = halos[u][s]
        return [functools.partial(third_stream, c, s) for s in range(3)]

    def third_stream(c, s):
        ats = [pl.ds(s * D + lanes(c, u), L) for u in range(U)]
        sums = [[None] * SHORT for _ in range(U)]
        for r in range(0, L, ROWS):
            marks = [bwd_mask[t - 1, r:r + ROWS] for t in range(1, SHORT)]
            for u in range(U):
                m = u * 3 + s
                x = qkv[r:r + ROWS, ats[u]].astype(F32)
                y = None
                for t in range(SHORT):
                    b = bg[c, m, r + t:r + t + ROWS]
                    if t:
                        b = b * marks[t - 1]
                    w = staps[t:t + 1, ats[u]] * b
                    y = w if y is None else y + w
                    p = x * b
                    p = functools.reduce(jnp.add, [p[k:k + 8] for k in range(0, ROWS, 8)])
                    sums[u][t] = p if sums[u][t] is None else sums[u][t] + p
                ig[r:r + ROWS, ats[u]] = y.astype(BF16)
        for u in range(U):
            terms = [jnp.sum(p, axis=0, keepdims=True) for p in sums[u]] + [jnp.zeros((1, L), F32)]
            grads[s * 4 + lax.rem(c, 2) * U + u, c // 2] = jnp.concatenate(terms, 0)

    def span(b):
        return pl.ds(*SPANS[b])

    def pairs(b):
        return pl.ds(SPANS[b][0] // 2, SPANS[b][1] // 2)

    def along(src, dst, s, r, k):
        return pltpu.make_async_remote_copy(src, dst, s, r, device_id=(lax.rem(dp + k, ndp), ctx), device_id_type=MESH)

    twin = dp + 1 - 2 * core
    mine = core * nz

    def twin_copy(b):
        src = grads.at[pl.ds(nz - mine, nz), span(b)]
        return pltpu.make_async_remote_copy(src, twin_in.at[:, span(b)], tsend.at[b], trecv.at[b], device_id=(twin, ctx), device_id_type=MESH)

    def z_copy(b, k, owner):
        return pltpu.make_async_remote_copy(grads.at[mine + owner, span(b)], z_in.at[k, span(b)], rsend.at[b, k], rrecv.at[b, k],
                                            device_id=(2 * lax.rem(z + k, nz) + core, ctx), device_id_type=MESH)

    def ag_all(b):
        block = total.at[pl.ds(1, ndp - 1), pairs(b)]
        return along(block, block, gsend.at[b], grecv.at[b], 1)

    def y_copy(b, k, slot):
        return hop(y_in.at[slot, span(b)], y_in.at[slot, span(b)], ysend.at[b, k], yrecv.at[b, k], y_at[k])

    def x_copy(b, k, slot):
        return hop(x_in.at[slot, span(b)], x_in.at[slot, span(b)], xsend.at[b, k], xrecv.at[b, k], x_at[k])

    def stage_a(b):
        twin_copy(b).start()

    def stage_b(b):
        twin_copy(b).wait_recv()
        both = grads[pl.ds(mine, nz), span(b)] + twin_in[:, span(b)]
        grads[pl.ds(mine, nz), span(b)] = both
        for k in range(1, nz):
            z_copy(b, k, lax.rem(z + k, nz)).start()

    def stage_c(b):
        acc = grads[mine + z, span(b)]
        for k in range(1, nz):
            z_copy(b, k, z).wait_recv()
            acc = acc + z_in[k, span(b)]
        y_in[my_y, span(b)] = acc
        for k in range(1, SIDE):
            y_copy(b, k, my_y).start()

    def stage_d(b):
        for k in range(1, SIDE):
            y_copy(b, k, lax.rem(my_y + SIDE - k, SIDE)).wait_recv()
        x_in[my_x, span(b)] = (y_in[0, span(b)] + y_in[1, span(b)]) + (y_in[2, span(b)] + y_in[3, span(b)])
        for k in range(1, SIDE):
            x_copy(b, k, my_x).start()

    def stage_e(b):
        for k in range(1, SIDE):
            x_copy(b, k, lax.rem(my_x + SIDE - k, SIDE)).wait_recv()
        summed = (x_in[0, span(b)] + x_in[1, span(b)]) + (x_in[2, span(b)] + x_in[3, span(b)])
        total[mine + z, pairs(b)] = summed.reshape(SPANS[b][1] // 2, 16, L).astype(BF16)

        def step(k, carry):
            block = total.at[mine + z, pairs(b)]
            along(block, block, gsend.at[b], grecv.at[b], k).start()
            return carry
        lax.fori_loop(1, ndp, step, 0)

    def take(c):
        @pl.when(lax.rem(c, PART) == 0)
        def _():
            prod_head(c // PART).wait_recv()
            gg_head(c // PART).wait_recv()

        prod_copy(c).wait_recv()
        gg_copy(c).wait_recv()

        @pl.when(c + AHEAD < CHUNKS)
        def _():
            prod_copy(c + AHEAD).start()
            gg_copy(c + AHEAD).start()

    def give(c):
        bg_copy(c).start()
        out_copy(c).start()

    def keep(c):
        for s in range(3):
            ig_copy(c, s).start()

    def ramp(c, carry):
        take(c)
        second(c)
        give(c)
        return carry

    def steady(c, carry):
        take(c)
        bg_copy(c - LAG).wait_recv()
        second(c)
        for unit in third(c - LAG):
            unit()
        give(c)
        keep(c - LAG)
        for when, stage, b in LOOP_STAGES:
            pl.when(c == when)(functools.partial(stages[stage], b))
        return carry

    stages = {"a": stage_a, "b": stage_b, "c": stage_c, "d": stage_d, "e": stage_e}
    lax.fori_loop(0, LAG, ramp, 0)
    lax.fori_loop(LAG, CHUNKS, steady, 0)

    def rest(c, carry):
        bg_copy(c).wait_recv()
        for unit in third(c):
            unit()
        keep(c)
        return carry

    stage_e(0)
    lax.fori_loop(CHUNKS - LAG, CHUNKS, rest, 0)
    for stage in stages.values():
        stage(1)
    for b in range(len(SPANS)):
        ag_all(b).wait_recv()
    for j in range(16):
        for pair in range(SUPER // 2):
            two = total[j, pair].astype(F32)
            for k in range(2):
                n = 4 * (2 * pair + k) + j % 4
                block = two[8 * k:8 * k + 8]
                if j < 12:
                    at = (j // 4) * D + n * L
                    sgo[:, at:at + L] = block[0:SHORT]
                else:
                    lag_all[8 * n:8 * n + 8] = block
    lgo[...] = lag_all[...].T

    for i in range(CHUNKS // PART):
        hq_copy(i).wait_send()
        prod_head(i).wait_send()
        gg_head(i).wait_send()

    def drain(c, carry):
        prod_copy(c).wait_send()
        gg_copy(c).wait_send()
        bg_copy(c).wait_send()
        out_copy(c).wait()
        for s in range(3):
            ig_copy(c, s).wait()
        return carry

    lax.fori_loop(0, CHUNKS, drain, 0)

    for b in range(len(SPANS)):
        twin_copy(b).wait_send()
        for k in range(1, nz):
            z_copy(b, k, lax.rem(z + k, nz)).wait_send()
        ag_all(b).wait_send()
        for k in range(1, SIDE):
            y_copy(b, k, my_y).wait_send()
            x_copy(b, k, my_x).wait_send()


def place(*refs):
    for i in range(4):
        refs[4 + i][...] = refs[i][...]


def body(nz, qkv, segments, short_taps, long_taps, cotangent):
    ndp = 2 * nz
    vmem = pl.BlockSpec(memory_space=pltpu.VMEM)
    anywhere = pl.BlockSpec(memory_space=pl.ANY)
    dma = pltpu.SemaphoreType.DMA
    shape = jax.ShapeDtypeStruct
    outs = (shape((L, D), BF16), shape((L, 3 * D), BF16), shape((SHORT, 3 * D), F32), shape((L, 8 * TILES), F32))
    results = pl.pallas_call(
        functools.partial(kernel, nz),
        out_shape=outs,
        in_specs=[pl.BlockSpec(memory_space=pltpu.HBM)] * 5,
        out_specs=[anywhere, anywhere, vmem, vmem],
        scratch_shapes=[
            pltpu.VMEM((L, 3 * D), BF16),
            pltpu.VMEM((1, 16 * L), jnp.int32),
            pltpu.VMEM((SHORT, 3 * D), F32),
            pltpu.VMEM((L, 8 * TILES), BF16),
            pltpu.VMEM((L, D), BF16),
            pltpu.VMEM((L, D), BF16),
            pltpu.VMEM((L, 3 * D), BF16),
            pltpu.VMEM((CHUNKS, 24 * U, L), BF16),
            pltpu.VMEM((CHUNKS, 24 * U, L), BF16),
            pltpu.VMEM((CHUNKS, 2 * L, W), BF16),
            pltpu.VMEM((CHUNKS, 2 * L, W), BF16),
            pltpu.VMEM((3, L, D), BF16),
            pltpu.VMEM((CHUNKS, 3 * U, L + 8, L), F32),
            pltpu.VMEM((CHUNKS, 24 * U, L), BF16),
            pltpu.VMEM((CHUNKS, 24 * U, L), BF16),
            pltpu.VMEM((3 * U, L, L), F32),
            pltpu.VMEM((3 * U, 8 + H, L), F32),
            pltpu.VMEM((SHORT - 1, L, L), F32),
            pltpu.VMEM((SHORT - 1, L, L), F32),
            pltpu.VMEM((L, 2 * L), BF16),
            pltpu.VMEM((L, 2 * L), BF16),
            pltpu.VMEM((2, L, L), F32),
            pltpu.VMEM((L + 16, L), F32),
            pltpu.VMEM((TILES, 8, L), F32),
            pltpu.VMEM((TILES, 8, L), F32),
            pltpu.VMEM((8, L, L), BF16),
            pltpu.VMEM((U, 8, 8, L), F32),
            pltpu.VMEM((8 * TILES, L), F32),
            pltpu.VMEM((ndp, SUPER, 8, L), F32),
            pltpu.VMEM((nz, SUPER, 8, L), F32),
            pltpu.VMEM((nz, SUPER, 8, L), F32),
            pltpu.VMEM((SIDE, SUPER, 8, L), F32),
            pltpu.VMEM((SIDE, SUPER, 8, L), F32),
            pltpu.VMEM((ndp, SUPER // 2, 16, L), BF16),
            dma((5,)), dma((4, CHUNKS)),
            dma((3, CHUNKS // PART)), dma((3, CHUNKS // PART)),
            dma((CHUNKS,)), dma((CHUNKS,)), dma((CHUNKS,)), dma((CHUNKS,)), dma((CHUNKS,)), dma((CHUNKS,)),
            dma((len(SPANS),)), dma((len(SPANS),)),
            dma((len(SPANS), nz)), dma((len(SPANS), nz)),
            dma((len(SPANS), SIDE)), dma((len(SPANS), SIDE)), dma((len(SPANS), SIDE)), dma((len(SPANS), SIDE)),
            dma((len(SPANS),)), dma((len(SPANS),)),
        ],
        compiler_params=pltpu.CompilerParams(collective_id=0, has_side_effects=True, vmem_limit_bytes=62 * 1024 * 1024),
        cost_estimate=pl.CostEstimate(flops=20_000_000_000, bytes_accessed=10_000_000, transcendentals=0),
        name="hyena",
    )(qkv[0], segments, short_taps, long_taps, cotangent[0])
    steps = 8
    specs = [pl.BlockSpec((L // steps, D), lambda i: (i, 0)), pl.BlockSpec((L // steps, 3 * D), lambda i: (i, 0)),
             pl.BlockSpec((SHORT, 3 * D // steps), lambda i: (0, i)), pl.BlockSpec((L // steps, 8 * TILES), lambda i: (i, 0))]
    out, ig, sg, lg = pl.pallas_call(
        place,
        grid=(steps,),
        out_shape=outs,
        in_specs=specs,
        out_specs=specs,
        name="place",
    )(*results)
    return out[None], ig[None], sg, lg


def solution(mesh):
    in_specs = (P("dp", "ctx", None), P("dp", None), P(), P(), P("dp", "ctx", None))
    out_specs = (P("dp", "ctx", None), P("dp", "ctx", None), P(), P())
    step = functools.partial(body, mesh.shape["dp"] // 2)
    return jax.shard_map(step, mesh=mesh, in_specs=in_specs, out_specs=out_specs, check_vma=False)
```

```python
import functools

import jax
import jax.numpy as jnp
from jax import lax
from jax.experimental import pallas as pl
from jax.experimental.pallas import tpu as pltpu
from jax.sharding import PartitionSpec as P

MESH = pl.DeviceIdType.MESH
L = 128
D = 4096
TILES = D // L
W = 256
CHUNKS = D // W
U = W // L
SHORT = 7
H = 16
SIDE = 4
SUPER = CHUNKS // 2
SPANS = ((0, 4), (4, 4))
LOOP_STAGES = ((11, "a", 0), (14, "b", 0))
STEPS = 4
PART = 4
EARLY = 8
AHEAD = 3
ROWS = 16
LAG = 4
F32 = jnp.float32
BF16 = jnp.bfloat16


def kernel(nz, qkv_hbm, segs_hbm, staps_hbm, ltaps_hbm, cot_hbm, out_hbm, ig_hbm, sgo, lgo,
           qkv, segs, staps, ltaps, cot, out, ig, hq_out, hq_in, prod, gg, short, bg, bg_out, bg_in, xs, xh, fwd_mask, bwd_mask,
           mf, mb, mtri, seg_col, hf, hb, lane_sel, lag_rows, lag_all,
           grads, twin_in, z_in, y_in, x_in, total,
           load, store, hsend, hrecv, psend, precv, csend, crecv, bsend, brecv, tsend, trecv, rsend, rrecv, ysend, yrecv, xsend, xrecv, gsend, grecv):
    nctx, ndp = SIDE * SIDE, 2 * nz
    dp, ctx = lax.axis_index("dp"), lax.axis_index("ctx")
    core, z = lax.rem(dp, 2), dp // 2
    left, right = lax.rem(ctx + nctx - 1, nctx), lax.rem(ctx + 1, nctx)
    my_x, my_y = ctx // SIDE, lax.rem(ctx, SIDE)
    y_at = [my_x * SIDE + lax.rem(my_y + k, SIDE) for k in range(SIDE)]
    x_at = [lax.rem(my_x + k, SIDE) * SIDE + my_y for k in range(SIDE)]

    loads = [pltpu.make_async_copy(src, dst, load.at[i]) for i, (src, dst) in enumerate(
        ((segs_hbm, segs), (ltaps_hbm, ltaps), (staps_hbm, staps), (qkv_hbm, qkv), (cot_hbm, cot)))]
    for one_load in loads:
        one_load.start()

    barrier = pltpu.get_barrier_semaphore()

    def greet_dp(k, c):
        pl.semaphore_signal(barrier, inc=1, device_id=(lax.rem(dp + k, ndp), ctx), device_id_type=MESH)
        return c

    lax.fori_loop(1, ndp, greet_dp, 0)
    for to in [left, right] + y_at[1:] + x_at[1:]:
        pl.semaphore_signal(barrier, inc=1, device_id=(dp, to), device_id_type=MESH)

    def hop(src, dst, s, r, to):
        return pltpu.make_async_remote_copy(src, dst, s, r, device_id=(dp, to), device_id_type=MESH)

    def part(i):
        return pl.ds(i * PART, PART)

    def hq_copy(i):
        return hop(hq_out.at[part(i)], hq_in.at[part(i)], hsend.at[0, i], hrecv.at[0, i], right)

    def prod_head(i):
        return hop(prod.at[part(i), pl.ds(L, H)], prod.at[part(i), pl.ds(0, H)], hsend.at[1, i], hrecv.at[1, i], right)

    def gg_head(i):
        return hop(gg.at[part(i), pl.ds(0, H)], gg.at[part(i), pl.ds(L, H)], hsend.at[2, i], hrecv.at[2, i], left)

    def prod_copy(c):
        return hop(prod.at[c, pl.ds(L + H, L - H)], prod.at[c, pl.ds(H, L - H)], psend.at[c], precv.at[c], right)

    def gg_copy(c):
        return hop(gg.at[c, pl.ds(H, L - H)], gg.at[c, pl.ds(L + H, L - H)], csend.at[c], crecv.at[c], left)

    def bg_copy(c):
        return hop(bg_out.at[c], bg_in.at[c], bsend.at[c], brecv.at[c], left)

    def out_copy(c):
        at = pl.ds(pl.multiple_of(c * W, W), W)
        return pltpu.make_async_copy(out.at[:, at], out_hbm.at[:, at], store.at[0, c])

    def ig_copy(c, s):
        at = pl.ds(pl.multiple_of(s * D + c * W, W), W)
        return pltpu.make_async_copy(ig.at[:, at], ig_hbm.at[:, at], store.at[1 + s, c])

    loads[0].wait()
    own = segs[0:1, pl.ds(pl.multiple_of(ctx * L, L), L)].astype(F32)
    prev = segs[0:1, pl.ds(pl.multiple_of(left * L, L), L)].astype(F32)
    nxt = segs[0:1, pl.ds(pl.multiple_of(right * L, L), L)].astype(F32)
    prev = jnp.where(ctx == 0, -1.0, prev)
    nxt = jnp.where(ctx == nctx - 1, -1.0, nxt)
    own_r = jnp.broadcast_to(own, (L, L))
    prev_r = jnp.broadcast_to(prev, (L, L))
    next_r = jnp.broadcast_to(nxt, (L, L))
    own_c = own_r.T
    seg_col[0:8] = prev_r.T[120:128]
    seg_col[8:136] = own_c
    seg_col[136:144] = next_r.T[0:8]
    rows = lax.broadcasted_iota(jnp.int32, (L, L), 0)
    cols = lax.broadcasted_iota(jnp.int32, (L, L), 1)
    same_own = own_c == own_r
    one = jnp.ones((L, L), F32)
    zero = jnp.zeros((L, L), F32)
    mf[:, 0:L] = jnp.where(jnp.logical_and(own_c == prev_r, rows < cols), one, zero).astype(BF16)
    mf[:, L:2 * L] = jnp.where(jnp.logical_and(same_own, rows >= cols), one, zero).astype(BF16)
    b_own = jnp.where(jnp.logical_and(same_own, cols >= rows), one, zero)
    b_next = jnp.where(jnp.logical_and(own_c == next_r, cols < rows), one, zero)
    mb[:, 0:L] = b_own.astype(BF16)
    mb[:, L:2 * L] = b_next.astype(BF16)
    mtri[0] = b_own
    mtri[1] = b_next
    for t in range(1, SHORT):
        fwd_mask[t - 1] = jnp.where(own_c == seg_col[8 - t:136 - t], one, zero)
        bwd_mask[t - 1] = jnp.where(own_c == seg_col[8 + t:136 + t], one, zero)
    loads[1].wait()
    eye = jnp.where(rows == cols, one, zero).astype(BF16)
    back = jnp.where(jnp.logical_or(rows + cols == L, rows + cols == 0), one, zero).astype(BF16)
    dims = (((0,), (0,)), ((), ()))
    hb[...] = lax.dot_general(ltaps[...], eye, dims, preferred_element_type=F32).reshape(TILES, 8, L)
    hf[...] = lax.dot_general(ltaps[...], back, dims, preferred_element_type=F32).reshape(TILES, 8, L)
    for g in range(8):
        lane_sel[g] = jnp.where(cols // 16 == g, one, zero).astype(BF16)
    lane_id = cols // 16

    for one_load in loads[2:]:
        one_load.wait()

    def pack(dst, c, parts):
        flat = [parts[u][s] for u in range(U) for s in range(3)]
        for k in range(0, 3 * U, 2):
            dst[c, 8 * k:8 * k + 16] = jnp.concatenate(flat[k:k + 2], 0).astype(BF16)

    def unpack(src, c):
        flat = []
        for k in range(0, 3 * U, 2):
            two = src[c, 8 * k:8 * k + 16].astype(F32)
            flat += [two[0:8], two[8:16]]
        return [flat[3 * u:3 * u + 3] for u in range(U)]

    def lanes(c, u):
        return pl.multiple_of(c * W + u * L, L)

    def pack_last(c, carry):
        pack(hq_out, c, [[qkv[L - 16:L, pl.ds(s * D + lanes(c, u), L)].astype(F32)[8:16] for s in range(3)] for u in range(U)])
        return carry

    lax.fori_loop(0, CHUNKS, pack_last, 0)

    def gates(c, u, r0, r1, done):
        here = slice(u * L, (u + 1) * L)
        wide = pl.ds(lanes(c, u), L)
        y = [d.astype(BF16) for d in done]
        for s in range(3):
            short[s, r0:r1, wide] = y[s]
        q, k, v = [d.astype(F32) for d in y]
        prod[c, L + r0:L + r1, here] = (k * v).astype(BF16)
        gg[c, r0:r1, here] = (cot[r0:r1, wide].astype(F32) * q).astype(BF16)

    def first(c, carry):
        for u in range(U):
            done = []
            for s in range(3):
                at = pl.ds(s * D + lanes(c, u), L)
                k = u * 3 + s
                x = qkv[:, at].astype(F32)
                xs[k] = x
                y = staps[0:1, at] * x[H:L]
                for t in range(1, SHORT):
                    y = y + staps[t:t + 1, at] * (xs[k, H - t:L - t] * fwd_mask[t - 1, H:L])
                done.append(y)
            gates(c, u, H, L, done)
        return carry

    lax.fori_loop(0, EARLY, first, 0)
    pl.semaphore_wait(barrier, ndp - 1 + 2 + 2 * (SIDE - 1))
    for i in range(CHUNKS // PART):
        hq_copy(i).start()
    for c in range(AHEAD):
        gg_copy(c).start()
    lax.fori_loop(EARLY, CHUNKS, first, 0)
    for c in range(AHEAD):
        prod_copy(c).start()

    def first_rows(c, carry):
        halos = unpack(hq_in, c)
        for u in range(U):
            done = []
            for s in range(3):
                at = pl.ds(s * D + lanes(c, u), L)
                k = u * 3 + s
                x = qkv[0:H, at].astype(F32)
                xh[k, 0:8] = halos[u][s]
                xh[k, 8:8 + H] = x
                y = staps[0:1, at] * x
                for t in range(1, SHORT):
                    y = y + staps[t:t + 1, at] * (xh[k, 8 - t:8 + H - t] * fwd_mask[t - 1, 0:H])
                done.append(y)
            gates(c, u, 0, H, done)
        return carry

    def first_part(i, carry):
        hq_copy(i).wait_recv()
        lax.fori_loop(i * PART, (i + 1) * PART, first_rows, 0)
        prod_head(i).start()
        gg_head(i).start()
        return carry

    lax.fori_loop(0, CHUNKS // PART, first_part, 0)

    def second(c):
        parts = []
        for u in range(U):
            here = slice(u * L, (u + 1) * L)
            n = c * U + u
            wide = pl.ds(lanes(c, u), L)
            p_ext = prod[c, :, here]
            g_ext = gg[c, :, here]
            p_own = p_ext[L:2 * L]
            taps_f = hf[n]
            taps_b = hb[n]
            mix = pg = None
            for g in range(8):
                rf = pltpu.roll(jnp.broadcast_to(taps_f[g:g + 1], (L, L)), 0, 1, stride=1, stride_axis=0).astype(BF16)
                rb = pltpu.roll(jnp.broadcast_to(taps_b[g:g + 1], (L, L)), 0, 1, stride=1, stride_axis=0).astype(BF16)
                lf = jnp.concatenate([rf * mf[:, 0:L], rf * mf[:, L:2 * L]], 1)
                lb = jnp.concatenate([rb * mb[:, 0:L], rb * mb[:, L:2 * L]], 1)
                r1 = jnp.dot(lf, p_ext, preferred_element_type=F32)
                r2 = jnp.dot(lb, g_ext, preferred_element_type=F32)
                rg = lax.dot_general(p_own * lane_sel[g], g_ext, (((1,), (1,)), ((), ())), preferred_element_type=F32)
                mix = r1 if mix is None else jnp.where(lane_id == g, r1, mix)
                pg = r2 if pg is None else jnp.where(lane_id == g, r2, pg)
                acc = None
                for k in range(16):
                    r = slice(8 * k, 8 * k + 8)
                    block = rg[r, 0:L] * mtri[0, r] + rg[r, L:2 * L] * mtri[1, r]
                    if k:
                        block = pltpu.roll(block, L - 8 * k, 1)
                    acc = block if acc is None else acc + block
                lag_rows[u, g] = acc
            lags = lag_rows[u, :, 0, :]
            for k in range(1, 8):
                lags = lags + pltpu.roll(lag_rows[u, :, k, :], L - k, 1)
            grads[12 + lax.rem(c, 2) * U + u, c // 2] = lags
            q = short[0, :, wide].astype(F32)
            k = short[1, :, wide].astype(F32)
            v = short[2, :, wide].astype(F32)
            out[:, wide] = (q * mix).astype(BF16)
            up = cot[:, wide].astype(F32)
            b = [x.astype(BF16).astype(F32) for x in (up * mix, pg * v, pg * k)]
            for s in range(3):
                bg[c, u * 3 + s, 0:L] = b[s]
            parts.append([x[0:8] for x in b])
        pack(bg_out, c, parts)

    def third(c):
        halos = unpack(bg_in, c)
        for u in range(U):
            for s in range(3):
                bg[c, u * 3 + s, L:L + 8] = halos[u][s]
        return [functools.partial(third_stream, c, s) for s in range(3)]

    def third_stream(c, s):
        ats = [pl.ds(s * D + lanes(c, u), L) for u in range(U)]
        sums = [[None] * SHORT for _ in range(U)]
        for r in range(0, L, ROWS):
            marks = [bwd_mask[t - 1, r:r + ROWS] for t in range(1, SHORT)]
            for u in range(U):
                m = u * 3 + s
                x = qkv[r:r + ROWS, ats[u]].astype(F32)
                y = None
                for t in range(SHORT):
                    b = bg[c, m, r + t:r + t + ROWS]
                    if t:
                        b = b * marks[t - 1]
                    w = staps[t:t + 1, ats[u]] * b
                    y = w if y is None else y + w
                    p = x * b
                    p = functools.reduce(jnp.add, [p[k:k + 8] for k in range(0, ROWS, 8)])
                    sums[u][t] = p if sums[u][t] is None else sums[u][t] + p
                ig[r:r + ROWS, ats[u]] = y.astype(BF16)
        for u in range(U):
            terms = [jnp.sum(p, axis=0, keepdims=True) for p in sums[u]] + [jnp.zeros((1, L), F32)]
            grads[s * 4 + lax.rem(c, 2) * U + u, c // 2] = jnp.concatenate(terms, 0)

    def span(b):
        return pl.ds(*SPANS[b])

    def along(src, dst, s, r, k):
        return pltpu.make_async_remote_copy(src, dst, s, r, device_id=(lax.rem(dp + k, ndp), ctx), device_id_type=MESH)

    twin = dp + 1 - 2 * core
    mine = core * nz

    def twin_copy(b):
        src = grads.at[pl.ds(nz - mine, nz), span(b)]
        return pltpu.make_async_remote_copy(src, twin_in.at[:, span(b)], tsend.at[b], trecv.at[b], device_id=(twin, ctx), device_id_type=MESH)

    def z_copy(b, k, owner):
        return pltpu.make_async_remote_copy(grads.at[mine + owner, span(b)], z_in.at[k, span(b)], rsend.at[b, k], rrecv.at[b, k],
                                            device_id=(2 * lax.rem(z + k, nz) + core, ctx), device_id_type=MESH)

    def total_copy(k):
        return along(total.at[mine + z], total.at[mine + z], gsend, grecv, k)

    def total_all():
        block = total.at[pl.ds(1, ndp - 1)]
        return along(block, block, gsend, grecv, 1)

    def y_copy(k, slot):
        return hop(y_in.at[slot], y_in.at[slot], ysend.at[k], yrecv.at[k], y_at[k])

    def x_copy(k, slot):
        return hop(x_in.at[slot], x_in.at[slot], xsend.at[k], xrecv.at[k], x_at[k])

    def stage_a(b):
        twin_copy(b).start()

    def stage_b(b):
        twin_copy(b).wait_recv()
        both = grads[pl.ds(mine, nz), span(b)] + twin_in[:, span(b)]
        grads[pl.ds(mine, nz), span(b)] = both
        for k in range(1, nz):
            z_copy(b, k, lax.rem(z + k, nz)).start()

    def stage_c():
        for b in range(len(SPANS)):
            acc = grads[mine + z, span(b)]
            for k in range(1, nz):
                z_copy(b, k, z).wait_recv()
                acc = acc + z_in[k, span(b)]
            y_in[my_y, span(b)] = acc
        for k in range(1, SIDE):
            y_copy(k, my_y).start()

    def stage_d():
        for k in range(1, SIDE):
            y_copy(k, lax.rem(my_y + SIDE - k, SIDE)).wait_recv()
        x_in[my_x] = (y_in[0] + y_in[1]) + (y_in[2] + y_in[3])
        for k in range(1, SIDE):
            x_copy(k, my_x).start()

    def stage_e():
        for k in range(1, SIDE):
            x_copy(k, lax.rem(my_x + SIDE - k, SIDE)).wait_recv()
        summed = (x_in[0] + x_in[1]) + (x_in[2] + x_in[3])
        total[mine + z] = summed.reshape(SUPER // 2, 16, L).astype(BF16)

        def step(k, carry):
            total_copy(k).start()
            return carry
        lax.fori_loop(1, ndp, step, 0)

    def take(c):
        @pl.when(lax.rem(c, PART) == 0)
        def _():
            prod_head(c // PART).wait_recv()
            gg_head(c // PART).wait_recv()

        prod_copy(c).wait_recv()
        gg_copy(c).wait_recv()

        @pl.when(c + AHEAD < CHUNKS)
        def _():
            prod_copy(c + AHEAD).start()
            gg_copy(c + AHEAD).start()

    def give(c):
        bg_copy(c).start()
        out_copy(c).start()

    def keep(c):
        for s in range(3):
            ig_copy(c, s).start()

    def ramp(c, carry):
        take(c)
        second(c)
        give(c)
        return carry

    def steady(c, carry):
        take(c)
        bg_copy(c - LAG).wait_recv()
        second(c)
        for unit in third(c - LAG):
            unit()
        give(c)
        keep(c - LAG)
        for when, stage, b in LOOP_STAGES:
            pl.when(c == when)(functools.partial(stages[stage], b))
        return carry

    stages = {"a": stage_a, "b": stage_b}
    lax.fori_loop(0, LAG, ramp, 0)
    lax.fori_loop(LAG, CHUNKS, steady, 0)

    def rest(c, carry):
        bg_copy(c).wait_recv()
        for unit in third(c):
            unit()
        keep(c)
        return carry

    lax.fori_loop(CHUNKS - LAG, CHUNKS, rest, 0)
    stage_a(1)
    stage_b(1)
    stage_c()
    stage_d()
    stage_e()
    total_all().wait_recv()
    for j in range(16):
        for pair in range(SUPER // 2):
            two = total[j, pair].astype(F32)
            for k in range(2):
                n = 4 * (2 * pair + k) + j % 4
                block = two[8 * k:8 * k + 8]
                if j < 12:
                    at = (j // 4) * D + n * L
                    sgo[:, at:at + L] = block[0:SHORT]
                else:
                    lag_all[8 * n:8 * n + 8] = block
    lgo[...] = lag_all[...].T

    for i in range(CHUNKS // PART):
        hq_copy(i).wait_send()
        prod_head(i).wait_send()
        gg_head(i).wait_send()

    def drain(c, carry):
        prod_copy(c).wait_send()
        gg_copy(c).wait_send()
        bg_copy(c).wait_send()
        out_copy(c).wait()
        for s in range(3):
            ig_copy(c, s).wait()
        return carry

    lax.fori_loop(0, CHUNKS, drain, 0)

    for b in range(len(SPANS)):
        twin_copy(b).wait_send()
        for k in range(1, nz):
            z_copy(b, k, lax.rem(z + k, nz)).wait_send()
    for k in range(1, SIDE):
        y_copy(k, my_y).wait_send()
        x_copy(k, my_x).wait_send()
    total_all().wait_send()


def place(out_in, ig_in, sg_in, lg_in, out, ig, sg, lg, out_v, ig_v, sg_v, lg_v, come, gone):
    moves = [(sg_in, sg_v, sg), (lg_in, lg_v, lg)]
    step = L // STEPS
    for i in range(STEPS):
        at = pl.ds(i * step, step)
        moves.append((ig_in.at[at], ig_v.at[at], ig.at[at]))
        moves.append((out_in.at[at], out_v.at[at], out.at[at]))
    ins = [pltpu.make_async_copy(m[0], m[1], come.at[i]) for i, m in enumerate(moves)]
    outs = [pltpu.make_async_copy(m[1], m[2], gone.at[i]) for i, m in enumerate(moves)]
    for move in ins:
        move.start()
    for i in range(len(moves)):
        ins[i].wait()
        outs[i].start()
    for move in outs:
        move.wait()


def body(nz, qkv, segments, short_taps, long_taps, cotangent):
    ndp = 2 * nz
    vmem = pl.BlockSpec(memory_space=pltpu.VMEM)
    anywhere = pl.BlockSpec(memory_space=pl.ANY)
    dma = pltpu.SemaphoreType.DMA
    shape = jax.ShapeDtypeStruct
    outs = (shape((L, D), BF16), shape((L, 3 * D), BF16), shape((SHORT, 3 * D), F32), shape((L, 8 * TILES), F32))
    results = pl.pallas_call(
        functools.partial(kernel, nz),
        out_shape=outs,
        in_specs=[pl.BlockSpec(memory_space=pltpu.HBM)] * 5,
        out_specs=[anywhere, anywhere, vmem, vmem],
        scratch_shapes=[
            pltpu.VMEM((L, 3 * D), BF16),
            pltpu.VMEM((1, 16 * L), jnp.int32),
            pltpu.VMEM((SHORT, 3 * D), F32),
            pltpu.VMEM((L, 8 * TILES), BF16),
            pltpu.VMEM((L, D), BF16),
            pltpu.VMEM((L, D), BF16),
            pltpu.VMEM((L, 3 * D), BF16),
            pltpu.VMEM((CHUNKS, 24 * U, L), BF16),
            pltpu.VMEM((CHUNKS, 24 * U, L), BF16),
            pltpu.VMEM((CHUNKS, 2 * L, W), BF16),
            pltpu.VMEM((CHUNKS, 2 * L, W), BF16),
            pltpu.VMEM((3, L, D), BF16),
            pltpu.VMEM((CHUNKS, 3 * U, L + 8, L), F32),
            pltpu.VMEM((CHUNKS, 24 * U, L), BF16),
            pltpu.VMEM((CHUNKS, 24 * U, L), BF16),
            pltpu.VMEM((3 * U, L, L), F32),
            pltpu.VMEM((3 * U, 8 + H, L), F32),
            pltpu.VMEM((SHORT - 1, L, L), F32),
            pltpu.VMEM((SHORT - 1, L, L), F32),
            pltpu.VMEM((L, 2 * L), BF16),
            pltpu.VMEM((L, 2 * L), BF16),
            pltpu.VMEM((2, L, L), F32),
            pltpu.VMEM((L + 16, L), F32),
            pltpu.VMEM((TILES, 8, L), F32),
            pltpu.VMEM((TILES, 8, L), F32),
            pltpu.VMEM((8, L, L), BF16),
            pltpu.VMEM((U, 8, 8, L), F32),
            pltpu.VMEM((8 * TILES, L), F32),
            pltpu.VMEM((ndp, SUPER, 8, L), F32),
            pltpu.VMEM((nz, SUPER, 8, L), F32),
            pltpu.VMEM((nz, SUPER, 8, L), F32),
            pltpu.VMEM((SIDE, SUPER, 8, L), F32),
            pltpu.VMEM((SIDE, SUPER, 8, L), F32),
            pltpu.VMEM((ndp, SUPER // 2, 16, L), BF16),
            dma((5,)), dma((4, CHUNKS)),
            dma((3, CHUNKS // PART)), dma((3, CHUNKS // PART)),
            dma((CHUNKS,)), dma((CHUNKS,)), dma((CHUNKS,)), dma((CHUNKS,)), dma((CHUNKS,)), dma((CHUNKS,)),
            dma((len(SPANS),)), dma((len(SPANS),)),
            dma((len(SPANS), nz)), dma((len(SPANS), nz)),
            dma((SIDE,)), dma((SIDE,)), dma((SIDE,)), dma((SIDE,)),
            dma, dma,
        ],
        compiler_params=pltpu.CompilerParams(collective_id=0, has_side_effects=True, vmem_limit_bytes=62 * 1024 * 1024),
        cost_estimate=pl.CostEstimate(flops=20_000_000_000, bytes_accessed=10_000_000, transcendentals=0),
        name="hyena",
    )(qkv[0], segments, short_taps, long_taps, cotangent[0])
    hbm = pl.BlockSpec(memory_space=pltpu.HBM)
    moves = 2 + 2 * STEPS
    out, ig, sg, lg = pl.pallas_call(
        place,
        out_shape=outs,
        in_specs=[hbm] * 4,
        out_specs=[hbm] * 4,
        scratch_shapes=[pltpu.VMEM(o.shape, o.dtype) for o in outs] + [dma((moves,)), dma((moves,))],
        name="place",
    )(*results)
    return out[None], ig[None], sg, lg


def solution(mesh):
    in_specs = (P("dp", "ctx", None), P("dp", None), P(), P(), P("dp", "ctx", None))
    out_specs = (P("dp", "ctx", None), P("dp", "ctx", None), P(), P())
    step = functools.partial(body, mesh.shape["dp"] // 2)
    return jax.shard_map(step, mesh=mesh, in_specs=in_specs, out_specs=out_specs, check_vma=False)
```

```python
import functools

import jax
import jax.numpy as jnp
from jax import lax
from jax.experimental import pallas as pl
from jax.experimental.pallas import tpu as pltpu
from jax.sharding import PartitionSpec as P

MESH = pl.DeviceIdType.MESH
L = 128
D = 4096
TILES = D // L
W = 256
CHUNKS = D // W
U = W // L
SHORT = 7
H = 16
SIDE = 4
SUPER = CHUNKS // 2
SPANS = ((0, 4), (4, 4))
LOOP_STAGES = ((11, "a", 0), (14, "b", 0))
STEPS = 4
PART = 2
READY = 2
EARLY = 4
AHEAD = 4
ROWS = 16
LAG = 4
F32 = jnp.float32
BF16 = jnp.bfloat16


def kernel(nz, qkv_hbm, segs_hbm, staps_hbm, ltaps_hbm, cot_hbm, out_hbm, ig_hbm, sgo, lgo,
           qkv, segs, staps, ltaps, cot, out, ig, hq_out, hq_in, prod, gg, short, bg, bg_out, bg_in, xs, xh, fwd_mask, bwd_mask,
           mf, mb, mtri, seg_col, hf, hb, lane_sel, lag_rows, lag_all,
           grads, twin_in, z_in, y_in, x_in, total,
           load, store, hsend, hrecv, psend, precv, csend, crecv, bsend, brecv, tsend, trecv, rsend, rrecv, ysend, yrecv, xsend, xrecv, gsend, grecv):
    nctx, ndp = SIDE * SIDE, 2 * nz
    dp, ctx = lax.axis_index("dp"), lax.axis_index("ctx")
    core, z = lax.rem(dp, 2), dp // 2
    left, right = lax.rem(ctx + nctx - 1, nctx), lax.rem(ctx + 1, nctx)
    my_x, my_y = ctx // SIDE, lax.rem(ctx, SIDE)
    y_at = [my_x * SIDE + lax.rem(my_y + k, SIDE) for k in range(SIDE)]
    x_at = [lax.rem(my_x + k, SIDE) * SIDE + my_y for k in range(SIDE)]

    loads = [pltpu.make_async_copy(src, dst, load.at[i]) for i, (src, dst) in enumerate(
        ((segs_hbm, segs), (ltaps_hbm, ltaps), (staps_hbm, staps), (qkv_hbm, qkv), (cot_hbm, cot)))]
    for one_load in loads:
        one_load.start()

    barrier = pltpu.get_barrier_semaphore()

    def greet_dp(k, c):
        pl.semaphore_signal(barrier, inc=1, device_id=(lax.rem(dp + k, ndp), ctx), device_id_type=MESH)
        return c

    lax.fori_loop(1, ndp, greet_dp, 0)
    for to in [left, right] + y_at[1:] + x_at[1:]:
        pl.semaphore_signal(barrier, inc=1, device_id=(dp, to), device_id_type=MESH)

    def hop(src, dst, s, r, to):
        return pltpu.make_async_remote_copy(src, dst, s, r, device_id=(dp, to), device_id_type=MESH)

    def part(i):
        return pl.ds(i * PART, PART)

    def hq_copy(i):
        return hop(hq_out.at[part(i)], hq_in.at[part(i)], hsend.at[0, i], hrecv.at[0, i], right)

    def prod_head(i):
        return hop(prod.at[part(i), pl.ds(L, H)], prod.at[part(i), pl.ds(0, H)], hsend.at[1, i], hrecv.at[1, i], right)

    def gg_head(i):
        return hop(gg.at[part(i), pl.ds(0, H)], gg.at[part(i), pl.ds(L, H)], hsend.at[2, i], hrecv.at[2, i], left)

    def prod_copy(c):
        return hop(prod.at[c, pl.ds(L + H, L - H)], prod.at[c, pl.ds(H, L - H)], psend.at[c], precv.at[c], right)

    def gg_copy(c):
        return hop(gg.at[c, pl.ds(H, L - H)], gg.at[c, pl.ds(L + H, L - H)], csend.at[c], crecv.at[c], left)

    def bg_copy(c):
        return hop(bg_out.at[c], bg_in.at[c], bsend.at[c], brecv.at[c], left)

    def out_copy(c):
        at = pl.ds(pl.multiple_of(c * W, W), W)
        return pltpu.make_async_copy(out.at[:, at], out_hbm.at[:, at], store.at[0, c])

    def ig_copy(c, s):
        at = pl.ds(pl.multiple_of(s * D + c * W, W), W)
        return pltpu.make_async_copy(ig.at[:, at], ig_hbm.at[:, at], store.at[1 + s, c])

    loads[0].wait()
    own = segs[0:1, pl.ds(pl.multiple_of(ctx * L, L), L)].astype(F32)
    prev = segs[0:1, pl.ds(pl.multiple_of(left * L, L), L)].astype(F32)
    nxt = segs[0:1, pl.ds(pl.multiple_of(right * L, L), L)].astype(F32)
    prev = jnp.where(ctx == 0, -1.0, prev)
    nxt = jnp.where(ctx == nctx - 1, -1.0, nxt)
    own_r = jnp.broadcast_to(own, (L, L))
    prev_r = jnp.broadcast_to(prev, (L, L))
    next_r = jnp.broadcast_to(nxt, (L, L))
    own_c = own_r.T
    seg_col[0:8] = prev_r.T[120:128]
    seg_col[8:136] = own_c
    seg_col[136:144] = next_r.T[0:8]
    rows = lax.broadcasted_iota(jnp.int32, (L, L), 0)
    cols = lax.broadcasted_iota(jnp.int32, (L, L), 1)
    same_own = own_c == own_r
    one = jnp.ones((L, L), F32)
    zero = jnp.zeros((L, L), F32)
    mf[:, 0:L] = jnp.where(jnp.logical_and(own_c == prev_r, rows < cols), one, zero).astype(BF16)
    mf[:, L:2 * L] = jnp.where(jnp.logical_and(same_own, rows >= cols), one, zero).astype(BF16)
    b_own = jnp.where(jnp.logical_and(same_own, cols >= rows), one, zero)
    b_next = jnp.where(jnp.logical_and(own_c == next_r, cols < rows), one, zero)
    mb[:, 0:L] = b_own.astype(BF16)
    mb[:, L:2 * L] = b_next.astype(BF16)
    mtri[0] = b_own
    mtri[1] = b_next
    for t in range(1, SHORT):
        fwd_mask[t - 1] = jnp.where(own_c == seg_col[8 - t:136 - t], one, zero)
        bwd_mask[t - 1] = jnp.where(own_c == seg_col[8 + t:136 + t], one, zero)
    loads[1].wait()
    eye = jnp.where(rows == cols, one, zero).astype(BF16)
    back = jnp.where(jnp.logical_or(rows + cols == L, rows + cols == 0), one, zero).astype(BF16)
    dims = (((0,), (0,)), ((), ()))
    hb[...] = lax.dot_general(ltaps[...], eye, dims, preferred_element_type=F32).reshape(TILES, 8, L)
    hf[...] = lax.dot_general(ltaps[...], back, dims, preferred_element_type=F32).reshape(TILES, 8, L)
    for g in range(8):
        lane_sel[g] = jnp.where(cols // 16 == g, one, zero).astype(BF16)
    lane_id = cols // 16

    for one_load in loads[2:]:
        one_load.wait()

    def pack(dst, c, parts):
        flat = [parts[u][s] for u in range(U) for s in range(3)]
        for k in range(0, 3 * U, 2):
            dst[c, 8 * k:8 * k + 16] = jnp.concatenate(flat[k:k + 2], 0).astype(BF16)

    def unpack(src, c):
        flat = []
        for k in range(0, 3 * U, 2):
            two = src[c, 8 * k:8 * k + 16].astype(F32)
            flat += [two[0:8], two[8:16]]
        return [flat[3 * u:3 * u + 3] for u in range(U)]

    def lanes(c, u):
        return pl.multiple_of(c * W + u * L, L)

    def pack_last(c, carry):
        pack(hq_out, c, [[qkv[L - 16:L, pl.ds(s * D + lanes(c, u), L)].astype(F32)[8:16] for s in range(3)] for u in range(U)])
        return carry

    lax.fori_loop(0, CHUNKS, pack_last, 0)

    def gates(c, u, r0, r1, done):
        here = slice(u * L, (u + 1) * L)
        wide = pl.ds(lanes(c, u), L)
        y = [d.astype(BF16) for d in done]
        for s in range(3):
            short[s, r0:r1, wide] = y[s]
        q, k, v = [d.astype(F32) for d in y]
        prod[c, L + r0:L + r1, here] = (k * v).astype(BF16)
        gg[c, r0:r1, here] = (cot[r0:r1, wide].astype(F32) * q).astype(BF16)

    def first(c, carry):
        for u in range(U):
            done = []
            for s in range(3):
                at = pl.ds(s * D + lanes(c, u), L)
                k = u * 3 + s
                x = qkv[:, at].astype(F32)
                xs[k] = x
                y = staps[0:1, at] * x[H:L]
                for t in range(1, SHORT):
                    y = y + staps[t:t + 1, at] * (xs[k, H - t:L - t] * fwd_mask[t - 1, H:L])
                done.append(y)
            gates(c, u, H, L, done)
        return carry

    lax.fori_loop(0, EARLY, first, 0)
    pl.semaphore_wait(barrier, ndp - 1 + 2 + 2 * (SIDE - 1))
    parts = CHUNKS // PART
    for i in range(READY):
        hq_copy(i).start()
    for c in range(AHEAD):
        gg_copy(c).start()
    middle = (EARLY + CHUNKS) // 2
    lax.fori_loop(EARLY, middle, first, 0)
    for i in range(READY, 2 * READY):
        hq_copy(i).start()
    prod_copy(0).start()
    lax.fori_loop(middle, CHUNKS, first, 0)
    for i in range(2 * READY, parts):
        hq_copy(i).start()

    def first_rows(c, carry):
        halos = unpack(hq_in, c)
        for u in range(U):
            done = []
            for s in range(3):
                at = pl.ds(s * D + lanes(c, u), L)
                k = u * 3 + s
                x = qkv[0:H, at].astype(F32)
                xh[k, 0:8] = halos[u][s]
                xh[k, 8:8 + H] = x
                y = staps[0:1, at] * x
                for t in range(1, SHORT):
                    y = y + staps[t:t + 1, at] * (xh[k, 8 - t:8 + H - t] * fwd_mask[t - 1, 0:H])
                done.append(y)
            gates(c, u, 0, H, done)
        return carry

    def first_part(i, carry):
        hq_copy(i).wait_recv()
        lax.fori_loop(i * PART, (i + 1) * PART, first_rows, 0)
        prod_head(i).start()
        gg_head(i).start()
        return carry

    lax.fori_loop(0, READY, first_part, 0)
    for c in range(1, AHEAD):
        prod_copy(c).start()

    def second(c):
        parts = []
        for u in range(U):
            here = slice(u * L, (u + 1) * L)
            n = c * U + u
            wide = pl.ds(lanes(c, u), L)
            p_ext = prod[c, :, here]
            g_ext = gg[c, :, here]
            p_own = p_ext[L:2 * L]
            taps_f = hf[n]
            taps_b = hb[n]
            mix = pg = None
            for g in range(8):
                rf = pltpu.roll(jnp.broadcast_to(taps_f[g:g + 1], (L, L)), 0, 1, stride=1, stride_axis=0).astype(BF16)
                rb = pltpu.roll(jnp.broadcast_to(taps_b[g:g + 1], (L, L)), 0, 1, stride=1, stride_axis=0).astype(BF16)
                lf = jnp.concatenate([rf * mf[:, 0:L], rf * mf[:, L:2 * L]], 1)
                lb = jnp.concatenate([rb * mb[:, 0:L], rb * mb[:, L:2 * L]], 1)
                r1 = jnp.dot(lf, p_ext, preferred_element_type=F32)
                r2 = jnp.dot(lb, g_ext, preferred_element_type=F32)
                rg = lax.dot_general(p_own * lane_sel[g], g_ext, (((1,), (1,)), ((), ())), preferred_element_type=F32)
                mix = r1 if mix is None else jnp.where(lane_id == g, r1, mix)
                pg = r2 if pg is None else jnp.where(lane_id == g, r2, pg)
                acc = None
                for k in range(16):
                    r = slice(8 * k, 8 * k + 8)
                    block = rg[r, 0:L] * mtri[0, r] + rg[r, L:2 * L] * mtri[1, r]
                    if k:
                        block = pltpu.roll(block, L - 8 * k, 1)
                    acc = block if acc is None else acc + block
                lag_rows[u, g] = acc
            lags = lag_rows[u, :, 0, :]
            for k in range(1, 8):
                lags = lags + pltpu.roll(lag_rows[u, :, k, :], L - k, 1)
            grads[12 + lax.rem(c, 2) * U + u, c // 2] = lags
            q = short[0, :, wide].astype(F32)
            k = short[1, :, wide].astype(F32)
            v = short[2, :, wide].astype(F32)
            out[:, wide] = (q * mix).astype(BF16)
            up = cot[:, wide].astype(F32)
            b = [x.astype(BF16).astype(F32) for x in (up * mix, pg * v, pg * k)]
            for s in range(3):
                bg[c, u * 3 + s, 0:L] = b[s]
            parts.append([x[0:8] for x in b])
        pack(bg_out, c, parts)

    def third(c):
        halos = unpack(bg_in, c)
        for u in range(U):
            for s in range(3):
                bg[c, u * 3 + s, L:L + 8] = halos[u][s]
        return [functools.partial(third_stream, c, s) for s in range(3)]

    def third_stream(c, s):
        ats = [pl.ds(s * D + lanes(c, u), L) for u in range(U)]
        sums = [[None] * SHORT for _ in range(U)]
        for r in range(0, L, ROWS):
            marks = [bwd_mask[t - 1, r:r + ROWS] for t in range(1, SHORT)]
            for u in range(U):
                m = u * 3 + s
                x = qkv[r:r + ROWS, ats[u]].astype(F32)
                y = None
                for t in range(SHORT):
                    b = bg[c, m, r + t:r + t + ROWS]
                    if t:
                        b = b * marks[t - 1]
                    w = staps[t:t + 1, ats[u]] * b
                    y = w if y is None else y + w
                    p = x * b
                    p = functools.reduce(jnp.add, [p[k:k + 8] for k in range(0, ROWS, 8)])
                    sums[u][t] = p if sums[u][t] is None else sums[u][t] + p
                ig[r:r + ROWS, ats[u]] = y.astype(BF16)
        for u in range(U):
            terms = [jnp.sum(p, axis=0, keepdims=True) for p in sums[u]] + [jnp.zeros((1, L), F32)]
            grads[s * 4 + lax.rem(c, 2) * U + u, c // 2] = jnp.concatenate(terms, 0)

    def span(b):
        return pl.ds(*SPANS[b])

    def along(src, dst, s, r, k):
        return pltpu.make_async_remote_copy(src, dst, s, r, device_id=(lax.rem(dp + k, ndp), ctx), device_id_type=MESH)

    twin = dp + 1 - 2 * core
    mine = core * nz

    def twin_copy(b):
        src = grads.at[pl.ds(nz - mine, nz), span(b)]
        return pltpu.make_async_remote_copy(src, twin_in.at[:, span(b)], tsend.at[b], trecv.at[b], device_id=(twin, ctx), device_id_type=MESH)

    def z_copy(b, k, owner):
        return pltpu.make_async_remote_copy(grads.at[mine + owner, span(b)], z_in.at[k, span(b)], rsend.at[b, k], rrecv.at[b, k],
                                            device_id=(2 * lax.rem(z + k, nz) + core, ctx), device_id_type=MESH)

    def total_copy(k):
        return along(total.at[mine + z], total.at[mine + z], gsend, grecv, k)

    def total_all():
        block = total.at[pl.ds(1, ndp - 1)]
        return along(block, block, gsend, grecv, 1)

    def y_copy(k, slot):
        return hop(y_in.at[slot], y_in.at[slot], ysend.at[k], yrecv.at[k], y_at[k])

    def x_copy(k, slot):
        return hop(x_in.at[slot], x_in.at[slot], xsend.at[k], xrecv.at[k], x_at[k])

    def stage_a(b):
        twin_copy(b).start()

    def stage_b(b):
        twin_copy(b).wait_recv()
        both = grads[pl.ds(mine, nz), span(b)] + twin_in[:, span(b)]
        grads[pl.ds(mine, nz), span(b)] = both
        for k in range(1, nz):
            z_copy(b, k, lax.rem(z + k, nz)).start()

    def stage_c():
        for b in range(len(SPANS)):
            acc = grads[mine + z, span(b)]
            for k in range(1, nz):
                z_copy(b, k, z).wait_recv()
                acc = acc + z_in[k, span(b)]
            y_in[my_y, span(b)] = acc
        for k in range(1, SIDE):
            y_copy(k, my_y).start()

    def stage_d():
        for k in range(1, SIDE):
            y_copy(k, lax.rem(my_y + SIDE - k, SIDE)).wait_recv()
        x_in[my_x] = (y_in[0] + y_in[1]) + (y_in[2] + y_in[3])
        for k in range(1, SIDE):
            x_copy(k, my_x).start()

    def stage_e():
        for k in range(1, SIDE):
            x_copy(k, lax.rem(my_x + SIDE - k, SIDE)).wait_recv()
        summed = (x_in[0] + x_in[1]) + (x_in[2] + x_in[3])
        total[mine + z] = summed.reshape(SUPER // 2, 16, L).astype(BF16)

        def step(k, carry):
            total_copy(k).start()
            return carry
        lax.fori_loop(1, ndp, step, 0)

    def take(c):
        @pl.when(jnp.logical_and(lax.rem(c, PART) == 0, c // PART + READY < parts))
        def _():
            first_part(c // PART + READY, 0)

        @pl.when(lax.rem(c, PART) == 0)
        def _():
            prod_head(c // PART).wait_recv()
            gg_head(c // PART).wait_recv()

        prod_copy(c).wait_recv()
        gg_copy(c).wait_recv()

        @pl.when(c + AHEAD < CHUNKS)
        def _():
            prod_copy(c + AHEAD).start()
            gg_copy(c + AHEAD).start()

    def give(c):
        bg_copy(c).start()
        out_copy(c).start()

    def keep(c):
        for s in range(3):
            ig_copy(c, s).start()

    def ramp(c, carry):
        take(c)
        second(c)
        give(c)
        return carry

    def steady(c, carry):
        take(c)
        bg_copy(c - LAG).wait_recv()
        second(c)
        for unit in third(c - LAG):
            unit()
        give(c)
        keep(c - LAG)
        for when, stage, b in LOOP_STAGES:
            pl.when(c == when)(functools.partial(stages[stage], b))
        return carry

    stages = {"a": stage_a, "b": stage_b}
    lax.fori_loop(0, LAG, ramp, 0)
    lax.fori_loop(LAG, CHUNKS, steady, 0)

    def rest(c, carry):
        bg_copy(c).wait_recv()
        for unit in third(c):
            unit()
        keep(c)
        return carry

    lax.fori_loop(CHUNKS - LAG, CHUNKS, rest, 0)
    stage_a(1)
    stage_b(1)
    stage_c()
    stage_d()
    stage_e()
    total_all().wait_recv()
    for j in range(16):
        for pair in range(SUPER // 2):
            two = total[j, pair].astype(F32)
            for k in range(2):
                n = 4 * (2 * pair + k) + j % 4
                block = two[8 * k:8 * k + 8]
                if j < 12:
                    at = (j // 4) * D + n * L
                    sgo[:, at:at + L] = block[0:SHORT]
                else:
                    lag_all[8 * n:8 * n + 8] = block
    lgo[...] = lag_all[...].T

    for i in range(CHUNKS // PART):
        hq_copy(i).wait_send()
        prod_head(i).wait_send()
        gg_head(i).wait_send()

    def drain(c, carry):
        prod_copy(c).wait_send()
        gg_copy(c).wait_send()
        bg_copy(c).wait_send()
        out_copy(c).wait()
        for s in range(3):
            ig_copy(c, s).wait()
        return carry

    lax.fori_loop(0, CHUNKS, drain, 0)

    for b in range(len(SPANS)):
        twin_copy(b).wait_send()
        for k in range(1, nz):
            z_copy(b, k, lax.rem(z + k, nz)).wait_send()
    for k in range(1, SIDE):
        y_copy(k, my_y).wait_send()
        x_copy(k, my_x).wait_send()
    total_all().wait_send()


def place(out_in, ig_in, sg_in, lg_in, out, ig, sg, lg, out_v, ig_v, sg_v, lg_v, come, gone):
    moves = [(sg_in, sg_v, sg), (lg_in, lg_v, lg)]
    step = L // STEPS
    for i in range(STEPS):
        at = pl.ds(i * step, step)
        moves.append((ig_in.at[at], ig_v.at[at], ig.at[at]))
        moves.append((out_in.at[at], out_v.at[at], out.at[at]))
    ins = [pltpu.make_async_copy(m[0], m[1], come.at[i]) for i, m in enumerate(moves)]
    outs = [pltpu.make_async_copy(m[1], m[2], gone.at[i]) for i, m in enumerate(moves)]
    for move in ins:
        move.start()
    for i in range(len(moves)):
        ins[i].wait()
        outs[i].start()
    for move in outs:
        move.wait()


def body(nz, qkv, segments, short_taps, long_taps, cotangent):
    ndp = 2 * nz
    vmem = pl.BlockSpec(memory_space=pltpu.VMEM)
    anywhere = pl.BlockSpec(memory_space=pl.ANY)
    dma = pltpu.SemaphoreType.DMA
    shape = jax.ShapeDtypeStruct
    outs = (shape((L, D), BF16), shape((L, 3 * D), BF16), shape((SHORT, 3 * D), F32), shape((L, 8 * TILES), F32))
    results = pl.pallas_call(
        functools.partial(kernel, nz),
        out_shape=outs,
        in_specs=[pl.BlockSpec(memory_space=pltpu.HBM)] * 5,
        out_specs=[anywhere, anywhere, vmem, vmem],
        scratch_shapes=[
            pltpu.VMEM((L, 3 * D), BF16),
            pltpu.VMEM((1, 16 * L), jnp.int32),
            pltpu.VMEM((SHORT, 3 * D), F32),
            pltpu.VMEM((L, 8 * TILES), BF16),
            pltpu.VMEM((L, D), BF16),
            pltpu.VMEM((L, D), BF16),
            pltpu.VMEM((L, 3 * D), BF16),
            pltpu.VMEM((CHUNKS, 24 * U, L), BF16),
            pltpu.VMEM((CHUNKS, 24 * U, L), BF16),
            pltpu.VMEM((CHUNKS, 2 * L, W), BF16),
            pltpu.VMEM((CHUNKS, 2 * L, W), BF16),
            pltpu.VMEM((3, L, D), BF16),
            pltpu.VMEM((CHUNKS, 3 * U, L + 8, L), F32),
            pltpu.VMEM((CHUNKS, 24 * U, L), BF16),
            pltpu.VMEM((CHUNKS, 24 * U, L), BF16),
            pltpu.VMEM((3 * U, L, L), F32),
            pltpu.VMEM((3 * U, 8 + H, L), F32),
            pltpu.VMEM((SHORT - 1, L, L), F32),
            pltpu.VMEM((SHORT - 1, L, L), F32),
            pltpu.VMEM((L, 2 * L), BF16),
            pltpu.VMEM((L, 2 * L), BF16),
            pltpu.VMEM((2, L, L), F32),
            pltpu.VMEM((L + 16, L), F32),
            pltpu.VMEM((TILES, 8, L), F32),
            pltpu.VMEM((TILES, 8, L), F32),
            pltpu.VMEM((8, L, L), BF16),
            pltpu.VMEM((U, 8, 8, L), F32),
            pltpu.VMEM((8 * TILES, L), F32),
            pltpu.VMEM((ndp, SUPER, 8, L), F32),
            pltpu.VMEM((nz, SUPER, 8, L), F32),
            pltpu.VMEM((nz, SUPER, 8, L), F32),
            pltpu.VMEM((SIDE, SUPER, 8, L), F32),
            pltpu.VMEM((SIDE, SUPER, 8, L), F32),
            pltpu.VMEM((ndp, SUPER // 2, 16, L), BF16),
            dma((5,)), dma((4, CHUNKS)),
            dma((3, CHUNKS // PART)), dma((3, CHUNKS // PART)),
            dma((CHUNKS,)), dma((CHUNKS,)), dma((CHUNKS,)), dma((CHUNKS,)), dma((CHUNKS,)), dma((CHUNKS,)),
            dma((len(SPANS),)), dma((len(SPANS),)),
            dma((len(SPANS), nz)), dma((len(SPANS), nz)),
            dma((SIDE,)), dma((SIDE,)), dma((SIDE,)), dma((SIDE,)),
            dma, dma,
        ],
        compiler_params=pltpu.CompilerParams(collective_id=0, has_side_effects=True, vmem_limit_bytes=62 * 1024 * 1024),
        cost_estimate=pl.CostEstimate(flops=20_000_000_000, bytes_accessed=10_000_000, transcendentals=0),
        name="hyena",
    )(qkv[0], segments, short_taps, long_taps, cotangent[0])
    hbm = pl.BlockSpec(memory_space=pltpu.HBM)
    moves = 2 + 2 * STEPS
    out, ig, sg, lg = pl.pallas_call(
        place,
        out_shape=outs,
        in_specs=[hbm] * 4,
        out_specs=[hbm] * 4,
        scratch_shapes=[pltpu.VMEM(o.shape, o.dtype) for o in outs] + [dma((moves,)), dma((moves,))],
        name="place",
    )(*results)
    return out[None], ig[None], sg, lg


def solution(mesh):
    in_specs = (P("dp", "ctx", None), P("dp", None), P(), P(), P("dp", "ctx", None))
    out_specs = (P("dp", "ctx", None), P("dp", "ctx", None), P(), P())
    step = functools.partial(body, mesh.shape["dp"] // 2)
    return jax.shard_map(step, mesh=mesh, in_specs=in_specs, out_specs=out_specs, check_vma=False)
```
